256 devices in a mesh: gx: 16 (over z, core), gy: 16 (over y, x).
Axes of the slice: x: 4, y: 4, z: 8, core: 2. Of those that a mesh axis runs over, the one named last changes fastest.
Arguments:
- right_side: float32 [128, 128, 8, 512], P('gx', 'gy'), may hold values from -9 to 9
- kappa_sq: float32 [128, 128, 512], P('gx', 'gy'), may hold values from 0.01 to 2
- coarse_inverse: float32 [4096, 256], P('gx'), may hold values from -0.25 to 32, as said below
Outputs:
- iterate: float32 [128, 128, 8, 512], P('gx', 'gy')
- residual: float32 [128, 128, 8, 512], P('gx', 'gy')
The draws below stay inside these ranges and needn't reach their ends.
Inputs may be any that keep to these rules, and one draw needn't show every extreme that they name: `coarse_inverse`: each slab's block of 256 rows is a symmetric 256 x 256 matrix; its off-diagonal entries lie within -0.25 to 0.25 and its diagonal entries within 8 to 32.
All inputs are finite; a program needn't handle non-finite values.
Results may differ from the reference program's by a relative error of at most 0.0003.
Values sent between devices are 32-bit elements; how exact they have to be, the bound alone decides.
No kernel may reach another device: no remote copies, remote signals or barrier semaphores. Data moves between devices by JAX's collectives and lax.ppermute only.
A program may use at most 64 MiB of HBM per device.

```python
import math
import jax
import jax.numpy as jnp
from jax import lax

CX = 8
CY = 8
NZ = 512
PROBES = 8
NCD = 16
ITERS = 2
NX = 128
NY = 128
COARSE = 256
N_GX = 16
N_GY = 16


def draw_right_side(key, part):
    key = jax.random.fold_in(key, 11)
    first_key = jax.random.fold_in(key, 0)
    shape = (NX, NY, PROBES, NZ)
    rows_x = (jnp.arange(NX, dtype=jnp.float32) + 0.5) / NX
    rows_y = (jnp.arange(NY, dtype=jnp.float32) + 0.5) / NY
    profile = (0.5 + rows_x)[:, None, None, None] * (0.8 + 0.4 * rows_y)[None, :, None, None]
    noise = jax.random.truncated_normal(first_key, -5.0, 5.0, shape, jnp.float32)
    return (noise * profile).astype(jnp.float32)


def draw_coarse_inverse(key, part):
    key = jax.random.fold_in(key, 23)
    first_key, second_key = jax.random.split(key)
    uniform_part = jax.random.uniform(first_key, (N_GX, COARSE, COARSE), jnp.float32, -1.0, 1.0)
    symmetric = 0.5 * (uniform_part + jnp.transpose(uniform_part, (0, 2, 1))) * 0.25
    diag_values = jnp.exp(jax.random.uniform(second_key, (N_GX, COARSE), jnp.float32, jnp.log(8.0), jnp.log(32.0)))
    index = jnp.arange(COARSE)
    identity = (index[:, None] == index[None, :]).astype(jnp.float32)
    matrix = symmetric * (1.0 - identity)[None] + diag_values[:, :, None] * identity[None]
    return matrix.reshape(N_GX * COARSE, COARSE).astype(jnp.float32)


def shard_levels(key, extent, cuts, smallest, largest):
    def one(dim, blocks):
        steps = jax.random.uniform(jax.random.fold_in(jax.random.fold_in(key, 6), dim), (blocks,), jnp.float32, smallest / len(cuts), largest / len(cuts))
        return jnp.repeat(jnp.exp(steps), extent[dim] // blocks).reshape((-1,) + (1,) * (len(extent) - dim - 1))

    loudness = one(*cuts[0])
    for cut in cuts[1:]:
        loudness = loudness * one(*cut)
    return loudness


def setup_inputs(seed: int = 0) -> dict:
    key_of = jax.random.split(jax.random.key(seed), 4)
    right_side = draw_right_side(jax.random.fold_in(key_of[3], 71), 0)
    kappa_sq = jnp.clip(jnp.exp(math.log(2.0) - 5.2983174 * jax.random.uniform(key_of[1], (NX, NY, NZ), jnp.float32) ** shard_levels(key_of[1], (NX, NY, NZ), ((0, 16), (1, 16)), -0.2, 0.2)), 0.01, 2.0)
    coarse_inverse = draw_coarse_inverse(jax.random.fold_in(key_of[3], 71), 0)
    return dict(right_side=right_side, kappa_sq=kappa_sq, coarse_inverse=coarse_inverse)


relax_weight = 2.0 / 3.0


def apply_operator(field, diag_shift):
    padded = jnp.pad(field, ((1, 1), (1, 1), (0, 0), (1, 1)))
    beside = padded[2:, 1:-1, :, 1:-1] + padded[:-2, 1:-1, :, 1:-1]
    beside = beside + padded[1:-1, 2:, :, 1:-1] + padded[1:-1, :-2, :, 1:-1]
    beside = beside + padded[1:-1, 1:-1, :, 2:] + padded[1:-1, 1:-1, :, :-2]
    return diag_shift * field - beside


def jacobi_sweep(correction, source, diag_shift):
    return correction + relax_weight * (source - apply_operator(correction, diag_shift)) / diag_shift


def coarse_correct(defect, coarse_inverse):
    zblock = NZ // NCD
    blocks = defect.reshape(N_GX, CX, N_GY, CY, PROBES, NCD, zblock)
    block_means = jnp.mean(blocks, axis=(1, 3, 6))
    panels = jnp.transpose(block_means, (0, 2, 1, 3)).reshape(N_GX, PROBES, COARSE)
    inverses = coarse_inverse.reshape(N_GX, COARSE, COARSE)
    values = jnp.einsum("gmn,gpn->gpm", inverses, panels, precision=lax.Precision.HIGHEST)
    values = jnp.transpose(values.reshape(N_GX, PROBES, N_GY, NCD), (0, 2, 1, 3))
    spread = jnp.broadcast_to(values[:, None, :, None, :, :, None], blocks.shape)
    return spread.reshape(defect.shape)


def precondition(source, diag_shift, coarse_inverse):
    correction = relax_weight * source / diag_shift
    correction = jacobi_sweep(correction, source, diag_shift)
    defect = source - apply_operator(correction, diag_shift)
    correction = correction + coarse_correct(defect, coarse_inverse)
    correction = jacobi_sweep(correction, source, diag_shift)
    return jacobi_sweep(correction, source, diag_shift)


def probe_dot(first, second):
    return jnp.sum(first * second, axis=(0, 1, 3))


def per_probe(values):
    return values[None, None, :, None]


def reference(right_side, kappa_sq, coarse_inverse):
    diag_shift = (6.0 + kappa_sq)[:, :, None, :]
    iterate = jnp.zeros_like(right_side)
    residual = right_side
    precond = precondition(residual, diag_shift, coarse_inverse)
    search = precond
    energy = probe_dot(residual, precond)
    for iteration in range(ITERS):
        op_image = apply_operator(search, diag_shift)
        step_size = energy / probe_dot(search, op_image)
        iterate = iterate + per_probe(step_size) * search
        residual = residual - per_probe(step_size) * op_image
        if iteration + 1 < ITERS:
            precond = precondition(residual, diag_shift, coarse_inverse)
            energy_next = probe_dot(residual, precond)
            search = precond + per_probe(energy_next / energy) * search
            energy = energy_next
    return iterate, residual
```

```python
import functools

import jax
import jax.numpy as jnp
from jax import lax
from jax.experimental import pallas as pl
from jax.experimental.pallas import tpu as pltpu
from jax.sharding import Mesh
from jax.sharding import PartitionSpec as P

OMEGA = 2.0 / 3.0
THIRD = 1.0 / 3.0
L = 128
CH = 4
HALO = 4
GX = ("z", "core")
SLAB2 = ("core", "gy")
ALL = ("z", "core", "gy")
CORNERS = ((-1, -1), (-1, 1), (1, -1), (1, 1))
HIGHEST = lax.Precision.HIGHEST


def lanes():
    return lax.broadcasted_iota(jnp.int32, (8, L), 1)


def ld(ref, x, y):
    return [ref[x, y, :, k * L : (k + 1) * L] for k in range(CH)]


def row(ref, x, y):
    return [jnp.broadcast_to(ref[x, pl.ds(y, 1), k * L : (k + 1) * L], (8, L)) for k in range(CH)]


def put(ref, x, y, values):
    for k in range(CH):
        ref[x, y, :, k * L : (k + 1) * L] = values[k]


def zsum(v, lane):
    up = [pltpu.roll(c, 1, 1) for c in v]
    down = [pltpu.roll(c, L - 1, 1) for c in v]
    out = []
    for k in range(CH):
        before = up[k - 1] if k > 0 else jnp.zeros_like(up[0])
        after = down[k + 1] if k < CH - 1 else jnp.zeros_like(up[0])
        out.append(jnp.where(lane == 0, before, up[k]) + jnp.where(lane == L - 1, after, down[k]))
    return out


def add(*terms):
    return [functools.reduce(lambda a, b: a + b, t) for t in zip(*terms)]


def mul(a, b):
    return [p * q for p, q in zip(a, b)]


def scale(s, a):
    return [s * p for p in a]


def join(v):
    return jnp.concatenate(v, axis=1)


def beside_rows(ref, x, lo, hi, lane):
    prev, here = ld(ref, x, lo - 1), ld(ref, x, lo)
    for y in range(lo, hi):
        after = ld(ref, x, y + 1)
        near = add(prev, after, ld(ref, x - 1, y), ld(ref, x + 1, y), zsum(here, lane))
        yield y, here, near
        prev, here = here, after


def shares(h_ref, source, g_own, g_faces, rows_ref):
    lane = lanes()
    zero = [jnp.zeros((8, L), jnp.float32)] * CH

    def one_row(i, carry):
        a1, ylo, yhi = carry
        total = zero
        for y, here, near in beside_rows(h_ref, i + 1, 1, 9, lane):
            j = y - 1
            t1 = add(scale(THIRD, source(i, j)), near)
            s = mul(g_own(i, j), t1)
            a1 = add(a1, t1)
            total = add(total, s)
            if j == 0:
                ylo = add(ylo, s)
            if j == 7:
                yhi = add(yhi, s)
        for k in range(CH):
            rows_ref[i, :, k * L : (k + 1) * L] = total[k]
        return a1, ylo, yhi

    a1, ylo, yhi = lax.fori_loop(0, 8, one_row, (zero, zero, zero))
    rows = [[rows_ref[i, :, k * L : (k + 1) * L] for k in range(CH)] for i in range(8)]
    s_all = add(*rows)
    edges = (rows[0], rows[7], ylo, yhi)
    faces = []
    for f, (cells, edge) in enumerate(
        zip(
            (
                [(1, j + 1) for j in range(8)],
                [(8, j + 1) for j in range(8)],
                [(i + 1, 1) for i in range(8)],
                [(i + 1, 8) for i in range(8)],
            ),
            edges,
        )
    ):
        t_sum, s_sum = zero, zero
        for n, (x, y) in enumerate(cells):
            t = ld(h_ref, x, y)
            s = mul(g_faces(f, n), t)
            t_sum, s_sum = add(t_sum, t), add(s_sum, s)
            if n == 0:
                first = s
            if n == 7:
                last = s
        part = add(
            scale(THIRD, t_sum),
            edge,
            scale(3.0, s_sum),
            scale(-1.0, add(first, last)),
            zsum(s_sum, lane),
        )
        faces.append((part, s_sum, first, last))
    (xl, sxl, xl0, xl7), (xh, sxh, xh0, xh7), (yl, syl, yl0, yl7), (yh, syh, yh0, yh7) = faces
    own = add(
        scale(THIRD, a1),
        scale(4.0, s_all),
        scale(-1.0, add(*edges)),
        sxl,
        sxh,
        syl,
        syh,
        zsum(s_all, lane),
    )
    parts = [
        add(xl0, yl0),
        xl,
        add(xl7, yh0),
        yl,
        own,
        yh,
        add(xh0, yl7),
        xh,
        add(xh7, yh7),
    ]
    stacked = jnp.concatenate([join(p) for p in parts], axis=0)
    zi = lax.broadcasted_iota(jnp.int32, (CH * L, L), 0)
    li = lax.broadcasted_iota(jnp.int32, (CH * L, L), 1)
    fold = jnp.where((zi // 32) == (li % 16), 1.0 / 2048.0, 0.0)
    sums = jnp.dot(stacked, fold, precision=HIGHEST, preferred_element_type=jnp.float32)
    r = lax.broadcasted_iota(jnp.int32, (8, L), 0)
    keep = (lane // 16) == r
    out = [
        jnp.sum(jnp.where(keep, sums[8 * n : 8 * n + 8], 0.0), axis=0, keepdims=True)
        for n in range(9)
    ]
    return jnp.concatenate(out, axis=0)


def fill_border(ref):
    zero = jnp.zeros((8, CH * L), jnp.float32)

    def one(i, carry):
        ref[0, i] = zero
        ref[9, i] = zero
        ref[i, 0] = zero
        ref[i, 9] = zero
        return carry

    lax.fori_loop(0, 10, one, 0)


def first_shares_kernel(b_ref, kap_ref, kxl, kxh, kyl, kyh, has_ref, out_ref, h_ref, g_ref, gf_ref, rows_ref):
    fill_border(h_ref)

    def one_row(i, carry):
        g_ref[i] = OMEGA / (6.0 + kap_ref[i])
        gf_ref[2, pl.ds(i, 1)] = OMEGA / (6.0 + kyl[i, 7:8]) * has_ref[2]
        gf_ref[3, pl.ds(i, 1)] = OMEGA / (6.0 + kyh[i, 0:1]) * has_ref[3]
        for j in range(8):
            put(h_ref, i + 1, j + 1, mul(row(g_ref, i, j), ld(b_ref, i, j)))
        return carry

    lax.fori_loop(0, 8, one_row, 0)
    gf_ref[0] = OMEGA / (6.0 + kxl[3]) * has_ref[0]
    gf_ref[1] = OMEGA / (6.0 + kxh[0]) * has_ref[1]
    out_ref[...] = shares(
        h_ref,
        lambda i, j: ld(b_ref, i, j),
        lambda i, j: row(g_ref, i, j),
        lambda f, n: row(gf_ref, f, n),
        rows_ref,
    )


def coarse_values(recv_ref, inv_ref, c_ref, count):
    lane = lanes()
    parts = []
    for t in range(3):
        total = jnp.zeros((48, L), jnp.float32)
        for j in range(count):
            value = None
            for dy in (-1, 0, 1):
                if not 0 <= j - dy < count:
                    continue
                for c in range(2):
                    term = recv_ref[c * count + j - dy, pl.ds(t * 3 + dy + 1, 1), :]
                    value = term if value is None else value + term
            total = total + inv_ref[t, j] * jnp.broadcast_to(value, (48, L))
        parts.append(total)
    r = lax.broadcasted_iota(jnp.int32, (8, L), 0)
    pick = jnp.where((lane // 16) == r, 1.0, 0.0)
    for t in range(3):
        c = lax.dot_general(
            pick,
            parts[t],
            (((1,), (1,)), ((), ())),
            precision=HIGHEST,
            preferred_element_type=jnp.float32,
        )
        for jj in range(3):
            for k in range(CH):
                out = jnp.zeros((8, L), jnp.float32)
                for q in range(4):
                    m = jj * 16 + k * 4 + q
                    out = jnp.where((lane // 32) == q, jnp.broadcast_to(c[:, m : m + 1], (8, L)), out)
                c_ref[t * 3 + jj, :, k * L : (k + 1) * L] = out


def cycle_kernel(first, count, *refs):
    (f_own, f_xl, f_xh, f_yl, f_yh, f_c0, f_c1, f_c2, f_c3, b_c0, b_c1, b_c2, b_c3) = refs[:13]
    kap_ref, kxl, kxh, kyl, kyh, has_ref, recv_ref, inv_ref = refs[13:21]
    refs = refs[21:]
    if first:
        z_ref, q_ref, dots_ref, out_ref = refs[:4]
        refs = refs[4:]
    else:
        extra_ref, earlier_ref, z_ref, q_ref, dots_ref = refs[:5]
        refs = refs[5:]
    F, A, B, G, KC, c_ref, h_ref, gf_ref, rows_ref, sems = refs
    n_sem = iter(range(64))
    copies = []

    def start(src, dst):
        copy = pltpu.make_async_copy(src, dst, sems.at[next(n_sem)])
        copy.start()
        copies.append(copy)

    for n, ref in enumerate((b_c0, b_c1, b_c2, b_c3)):
        start(ref.at[6:9], KC.at[n])
    start(f_own, F.at[4:12, 4:12])
    start(f_xl, F.at[0:4, 4:12])
    start(f_xh, F.at[12:16, 4:12])
    start(f_yl, F.at[4:12, 0:4])
    start(f_yh, F.at[4:12, 12:16])
    for (sx, sy), ref in zip(CORNERS, (f_c0, f_c1, f_c2, f_c3)):
        at = 0
        for a in (1, 2, 3):
            wide = 4 - a
            x = 4 - a if sx < 0 else 11 + a
            y = 4 - wide if sy < 0 else 12
            start(ref.at[at : at + wide], F.at[x, y : y + wide])
            at += wide

    zero = jnp.zeros((8, CH * L), jnp.float32)
    for x, y in [(a, b) for a in range(4) for b in range(4) if (4 - a) + (4 - b) > 4]:
        for xx, yy in ((x, y), (x, 15 - y), (15 - x, y), (15 - x, 15 - y)):
            F[xx, yy] = zero

    def inv_diag(kappa):
        return OMEGA / (6.0 + kappa)

    coarse_values(recv_ref, inv_ref, c_ref, count)

    for copy in copies[:4]:
        copy.wait()
    for i in range(8):
        G[4 + i, 8:16] = inv_diag(kap_ref[i])
        G[4 + i, 0:8] = inv_diag(kyl[i]) * has_ref[2]
        G[4 + i, 16:24] = inv_diag(kyh[i]) * has_ref[3]
    for a in range(4):
        G[a, 8:16] = inv_diag(kxl[a]) * has_ref[0]
        G[12 + a, 8:16] = inv_diag(kxh[a]) * has_ref[1]
    for n, (sx, sy) in enumerate(CORNERS):
        mask = has_ref[0 if sx < 0 else 1] * has_ref[2 if sy < 0 else 3]
        y = 0 if sy < 0 else 16
        G[0 if sx < 0 else 15, y : y + 8] = zero
        for a in (1, 2, 3):
            x = 4 - a if sx < 0 else 11 + a
            G[x, y : y + 8] = inv_diag(KC[n, a - 1]) * mask
    for copy in copies[4:]:
        copy.wait()

    lane = lanes()

    def start_row(x, carry):
        for y in range(16):
            put(A, x, y, mul(row(G, x, y + 4), ld(F, x, y)))
        return carry

    lax.fori_loop(0, 16, start_row, 0)

    def sweep(src, dst, edge, coarse):
        def one_row(x, carry):
            t = jnp.where(x >= 4, 1, 0) + jnp.where(x >= 12, 1, 0)
            for y, here, near in beside_rows(src, x, edge, 16 - edge, lane):
                new = add(scale(THIRD, here), mul(add(ld(F, x, y), near), row(G, x, y + 4)))
                if coarse:
                    jj = (1 if y >= 4 else 0) + (1 if y >= 12 else 0)
                    new = add(new, [c_ref[t * 3 + jj, :, k * L : (k + 1) * L] for k in range(CH)])
                put(dst, x, y, new)
            return carry

        lax.fori_loop(edge, 16 - edge, one_row, 0)

    sweep(A, B, 1, True)
    sweep(B, A, 2, False)
    sweep(A, B, 3, False)
    if first:
        fill_border(h_ref)
    nil = jnp.zeros((8, L), jnp.float32)

    def image_row(i, carry):
        fz, zq, ez = carry
        x = i + 4
        for y, here, near in beside_rows(B, x, 4, 12, lane):
            j = y - 4
            kappa = row(kap_ref, i, j)
            image = [(6.0 + kappa[k]) * here[k] - near[k] for k in range(CH)]
            put(z_ref, i, j, here)
            put(q_ref, i, j, image)
            source = ld(F, x, y)
            fz = functools.reduce(lambda a, b: a + b, mul(source, here), fz)
            zq = functools.reduce(lambda a, b: a + b, mul(here, image), zq)
            if first:
                put(h_ref, i + 1, j + 1, mul(row(G, x, y + 4), image))
            else:
                ez = functools.reduce(lambda a, b: a + b, mul(ld(extra_ref, i, j), here), ez)
        return fz, zq, ez

    fz, zq, ez = lax.fori_loop(0, 8, image_row, (nil, nil, nil))
    if first:
        dots_ref[0] = fz
        dots_ref[1] = zq
        gf_ref[0] = G[3, 8:16]
        gf_ref[1] = G[12, 8:16]
        for i in range(8):
            gf_ref[2, pl.ds(i, 1)] = G[4 + i, 7:8]
            gf_ref[3, pl.ds(i, 1)] = G[4 + i, 16:17]
        out_ref[...] = shares(
            h_ref,
            lambda i, j: ld(q_ref, i, j),
            lambda i, j: row(G, i + 4, j + 8),
            lambda f, n: row(gf_ref, f, n),
            rows_ref,
        )
    else:
        total = [earlier_ref[0], earlier_ref[1], fz, zq, ez]
        packed = nil
        for k, part in enumerate(total):
            packed = jnp.where(lane == k, jnp.sum(part, axis=1, keepdims=True), packed)
        dots_ref[...] = packed


def combine_kernel(sums_ref, b_ref, z_ref, q_ref, w_ref, v_ref, x_ref, r_ref):
    sums = sums_ref[0]
    for n in range(1, sums_ref.shape[0]):
        sums = sums + sums_ref[n]
    bz, zq, qw, wv, bw = (sums[:, k : k + 1] for k in range(5))
    a0 = bz / zq
    e1 = bz - a0 * (bw + zq) + a0 * a0 * qw
    beta = e1 / bz
    z1q = zq - a0 * qw
    z1v = zq - 2.0 * a0 * qw + a0 * a0 * wv
    a1 = e1 / (z1v + 2.0 * beta * z1q + beta * beta * zq)
    cz = a0 + a1 * (1.0 + beta)
    cw = a1 * a0
    cz = jnp.broadcast_to(cz, (8, CH * L))
    cw = jnp.broadcast_to(cw, (8, CH * L))
    for i in range(x_ref.shape[0]):
        for j in range(x_ref.shape[1]):
            x_ref[i, j] = cz * z_ref[i, j] - cw * w_ref[i, j]
            r_ref[i, j] = b_ref[i, j] - cz * q_ref[i, j] + cw * v_ref[i, j]


def shift(value, axes, sizes, steps):
    pairs = []
    total = 1
    for n in sizes:
        total *= n
    for flat in range(total):
        rest, target = flat, 0
        weight = 1
        for n, step in zip(reversed(sizes), reversed(steps)):
            at = rest % n
            rest //= n
            target += ((at + step) % n) * weight
            weight *= n
        pairs.append((flat, target))
    return lax.ppermute(value, axes, pairs)


def corner_cells(field, sx, sy):
    pieces = []
    for a in (1, 2, 3):
        x = 8 - a if sx > 0 else a - 1
        wide = 4 - a
        y = 8 - wide if sy > 0 else 0
        pieces.append(field[x, y : y + wide])
    return pieces


def corner_rows(kappa, sx):
    return kappa[5:8][::-1] if sx > 0 else kappa[0:3]


VM = pl.BlockSpec(memory_space=pltpu.VMEM)
SM = pl.BlockSpec(memory_space=pltpu.SMEM)
HB = pl.BlockSpec(memory_space=pl.ANY)


def solution(mesh):
    n_gx, n_gy = mesh.shape["gx"], mesh.shape["gy"]
    n_z = n_gx // 2
    fine = Mesh(mesh.devices.reshape(n_z, 2, n_gy), ALL)

    def halo(field):
        xl = shift(field[4:8], GX, (n_gx,), (1,))
        xh = shift(field[0:4], GX, (n_gx,), (-1,))
        yl = shift(field[:, 4:8], ("gy",), (n_gy,), (1,))
        yh = shift(field[:, 0:4], ("gy",), (n_gy,), (-1,))
        return [xl, xh, yl, yh]

    def corners(field, kappa):
        out = []
        for sx, sy in CORNERS:
            pieces = corner_cells(field, -sx, -sy)
            if kappa is not None:
                pieces.append(corner_rows(kappa, -sx))
            packed = jnp.concatenate(pieces, axis=0)
            out.append(shift(packed, ALL, (n_gx, n_gy), (-sx, -sy)))
        return out

    def gather_shares(own, z, core):
        low = shift(own, ("z",), (n_z,), (1,)).reshape(3, 3, L)
        high = shift(own, ("z",), (n_z,), (-1,)).reshape(3, 3, L)
        low = jnp.where(z > 0, low, 0.0)
        high = jnp.where(z < n_z - 1, high, 0.0)
        own = own.reshape(3, 3, L)
        none = jnp.zeros((1, 3, L), jnp.float32)
        even = jnp.concatenate([own[0:1] + low[2:3], own[1:2], own[2:3] + high[0:1], high[1:2]])
        odd = jnp.concatenate([low[1:2], own[0:1] + low[2:3], own[1:2], own[2:3] + high[0:1]])
        total = jnp.where(core == 0, even, odd)
        to_even = jnp.broadcast_to(total[0:3].reshape(1, 9, L), (n_gy, 9, L))
        to_odd = jnp.broadcast_to(total[1:4].reshape(1, 9, L), (n_gy, 9, L))
        return lax.all_to_all(jnp.concatenate([to_even, to_odd]), SLAB2, 0, 0)

    def body(b, kappa, inverse):
        f32 = jnp.float32
        z, core, gy = lax.axis_index("z"), lax.axis_index("core"), lax.axis_index("gy")
        gx = z * 2 + core
        has = jnp.stack([gx > 0, gx < n_gx - 1, gy > 0, gy < n_gy - 1]).astype(f32)

        kxl, kxh, kyl, kyh = (
            shift(kappa[4:8], GX, (n_gx,), (1,)),
            shift(kappa[0:4], GX, (n_gx,), (-1,)),
            shift(kappa, ("gy",), (n_gy,), (1,)),
            shift(kappa, ("gy",), (n_gy,), (-1,)),
        )
        first_own = pl.pallas_call(
            first_shares_kernel,
            out_shape=jax.ShapeDtypeStruct((9, L), f32),
            in_specs=[VM] * 6 + [SM],
            out_specs=VM,
            scratch_shapes=[
                pltpu.VMEM((10, 10, 8, CH * L), f32),
                pltpu.VMEM((8, 8, CH * L), f32),
                pltpu.VMEM((4, 8, CH * L), f32),
                pltpu.VMEM((8, 8, CH * L), f32),
            ],
            compiler_params=pltpu.CompilerParams(vmem_limit_bytes=20 << 20),
            name="first_shares",
        )(b, kappa, kxl, kxh, kyl, kyh, has)

        near = jnp.pad(inverse, ((16, 16), (0, 0)))
        near = lax.dynamic_slice_in_dim(near, gy * 16, 48, 0)
        near_low = shift(near, GX, (n_gx,), (1,)) * has[0]
        near_high = shift(near, GX, (n_gx,), (-1,)) * has[1]
        inv = jnp.stack([near_low, near, near_high]).reshape(3, 48, n_gy, 16)
        inv = jnp.tile(jnp.transpose(inv, (0, 2, 1, 3)), (1, 1, 1, 8))

        b_halo = halo(b)
        b_corners = corners(b, kappa)

        def cycle(first, field, faces, diagonals, received, more):
            tile = jax.ShapeDtypeStruct((8, 8, 8, CH * L), f32)
            outs = [tile, tile]
            if first:
                outs += [jax.ShapeDtypeStruct((2, 8, L), f32), jax.ShapeDtypeStruct((9, L), f32)]
            else:
                outs += [jax.ShapeDtypeStruct((8, L), f32)]
            big = pltpu.VMEM((16, 16, 8, CH * L), f32)
            return pl.pallas_call(
                functools.partial(cycle_kernel, first, n_gy),
                out_shape=outs,
                in_specs=[HB] * 13 + [VM] * 5 + [SM] + [VM] * (2 + len(more)),
                out_specs=[VM] * len(outs),
                scratch_shapes=[
                    big,
                    big,
                    big,
                    pltpu.VMEM((16, 24, CH * L), f32),
                    pltpu.VMEM((4, 3, 8, CH * L), f32),
                    pltpu.VMEM((9, 8, CH * L), f32),
                    pltpu.VMEM((10, 10, 8, CH * L), f32),
                    pltpu.VMEM((4, 8, CH * L), f32),
                    pltpu.VMEM((8, 8, CH * L), f32),
                    pltpu.SemaphoreType.DMA((24,)),
                ],
                compiler_params=pltpu.CompilerParams(vmem_limit_bytes=40 << 20),
                name="first_cycle" if first else "second_cycle",
            )(field, *faces, *diagonals, *b_corners, kappa, kxl, kxh, kyl, kyh, has, received, inv, *more)

        received = gather_shares(first_own, z, core)
        z0, q0, dots, own = cycle(True, b, b_halo, b_corners, received, [])
        q_halo = halo(q0)
        q_corners = corners(q0, None)
        received = gather_shares(own, z, core)
        w0, v0, packed = cycle(False, q0, q_halo, q_corners, received, [b, dots])

        near_sum = jnp.sum(
            lax.all_to_all(jnp.broadcast_to(packed, (2 * n_gy, 8, L)), SLAB2, 0, 0), axis=0
        )
        sums = lax.all_to_all(jnp.broadcast_to(near_sum, (n_z, 8, L)), "z", 0, 0)
        tile = pl.BlockSpec((1, 8, 8, CH * L), lambda i: (i, 0, 0, 0))
        return pl.pallas_call(
            combine_kernel,
            grid=(8,),
            out_shape=[jax.ShapeDtypeStruct((8, 8, 8, CH * L), f32)] * 2,
            in_specs=[pl.BlockSpec((n_z, 8, L), lambda i: (0, 0, 0))] + [tile] * 5,
            out_specs=[tile, tile],
            name="combine",
        )(sums, b, z0, q0, w0, v0)

    field = P(GX, "gy", None, None)
    return jax.shard_map(
        body,
        mesh=fine,
        in_specs=(field, P(GX, "gy", None), P(GX, None)),
        out_specs=(field, field),
        check_vma=False,
    )
```

```python
import functools

import jax
import jax.numpy as jnp
from jax import lax
from jax.experimental import pallas as pl
from jax.experimental.pallas import tpu as pltpu
from jax.sharding import Mesh
from jax.sharding import PartitionSpec as P

OMEGA = 2.0 / 3.0
THIRD = 1.0 / 3.0
L = 128
CH = 4
HALO = 4
GX = ("z", "core")
SLAB2 = ("core", "gy")
ALL = ("z", "core", "gy")
HIGHEST = lax.Precision.HIGHEST
WHOLE = pltpu.CompilerParams(vmem_limit_bytes=(64 << 20) - (64 << 10))
GRANT = pltpu.CompilerParams(vmem_limit_bytes=(63 << 20) + (256 << 10))


def lanes():
    return lax.broadcasted_iota(jnp.int32, (8, L), 1)


def ld(ref, x, y):
    return [ref[x, y, :, k * L : (k + 1) * L] for k in range(CH)]


def row(ref, x, y):
    return [jnp.broadcast_to(ref[x, pl.ds(y, 1), k * L : (k + 1) * L], (8, L)) for k in range(CH)]


def put(ref, x, y, values):
    for k in range(CH):
        ref[x, y, :, k * L : (k + 1) * L] = values[k]


def zsum(v, lane):
    up = [pltpu.roll(c, 1, 1) for c in v]
    down = [pltpu.roll(c, L - 1, 1) for c in v]
    out = []
    for k in range(CH):
        before = up[k - 1] if k > 0 else jnp.zeros_like(up[0])
        after = down[k + 1] if k < CH - 1 else jnp.zeros_like(up[0])
        out.append(jnp.where(lane == 0, before, up[k]) + jnp.where(lane == L - 1, after, down[k]))
    return out


def add(*terms):
    return [functools.reduce(lambda a, b: a + b, t) for t in zip(*terms)]


def mul(a, b):
    return [p * q for p, q in zip(a, b)]


def scale(s, a):
    return [s * p for p in a]


def join(v):
    return jnp.concatenate(v, axis=1)


def beside_rows(ref, x, lo, hi, lane):
    prev, here = ld(ref, x, lo - 1), ld(ref, x, lo)
    for y in range(lo, hi):
        after = ld(ref, x, y + 1)
        near = add(prev, after, ld(ref, x - 1, y), ld(ref, x + 1, y), zsum(here, lane))
        yield y, here, near
        prev, here = here, after


def shares(h_ref, source, g_own, g_faces, rows_ref):
    lane = lanes()
    zero = [jnp.zeros((8, L), jnp.float32)] * CH

    def one_row(i, carry):
        a1, ylo, yhi = carry
        total = zero
        for y, here, near in beside_rows(h_ref, i + 1, 1, 9, lane):
            j = y - 1
            t1 = add(scale(THIRD, source(i, j)), near)
            s = mul(g_own(i, j), t1)
            a1 = add(a1, t1)
            total = add(total, s)
            if j == 0:
                ylo = add(ylo, s)
            if j == 7:
                yhi = add(yhi, s)
        for k in range(CH):
            rows_ref[i, :, k * L : (k + 1) * L] = total[k]
        return a1, ylo, yhi

    a1, ylo, yhi = lax.fori_loop(0, 8, one_row, (zero, zero, zero))
    rows = [[rows_ref[i, :, k * L : (k + 1) * L] for k in range(CH)] for i in range(8)]
    s_all = add(*rows)
    edges = (rows[0], rows[7], ylo, yhi)
    faces = []
    for f, (cells, edge) in enumerate(
        zip(
            (
                [(1, j + 1) for j in range(8)],
                [(8, j + 1) for j in range(8)],
                [(i + 1, 1) for i in range(8)],
                [(i + 1, 8) for i in range(8)],
            ),
            edges,
        )
    ):
        t_sum, s_sum = zero, zero
        for n, (x, y) in enumerate(cells):
            t = ld(h_ref, x, y)
            s = mul(g_faces(f, n), t)
            t_sum, s_sum = add(t_sum, t), add(s_sum, s)
            if n == 0:
                first = s
            if n == 7:
                last = s
        part = add(
            scale(THIRD, t_sum),
            edge,
            scale(3.0, s_sum),
            scale(-1.0, add(first, last)),
            zsum(s_sum, lane),
        )
        faces.append((part, s_sum, first, last))
    (xl, sxl, xl0, xl7), (xh, sxh, xh0, xh7), (yl, syl, yl0, yl7), (yh, syh, yh0, yh7) = faces
    own = add(
        scale(THIRD, a1),
        scale(4.0, s_all),
        scale(-1.0, add(*edges)),
        sxl,
        sxh,
        syl,
        syh,
        zsum(s_all, lane),
    )
    parts = [
        add(xl0, yl0),
        xl,
        add(xl7, yh0),
        yl,
        own,
        yh,
        add(xh0, yl7),
        xh,
        add(xh7, yh7),
    ]
    stacked = jnp.concatenate([join(p) for p in parts], axis=0)
    zi = lax.broadcasted_iota(jnp.int32, (CH * L, L), 0)
    li = lax.broadcasted_iota(jnp.int32, (CH * L, L), 1)
    fold = jnp.where((zi // 32) == (li % 16), 1.0 / 2048.0, 0.0)
    sums = jnp.dot(stacked, fold, precision=HIGHEST, preferred_element_type=jnp.float32)
    r = lax.broadcasted_iota(jnp.int32, (8, L), 0)
    keep = (lane // 16) == r
    out = [
        jnp.sum(jnp.where(keep, sums[8 * n : 8 * n + 8], 0.0), axis=0, keepdims=True)
        for n in range(9)
    ]
    return jnp.concatenate(out, axis=0)


def fill_border(ref):
    zero = jnp.zeros((8, CH * L), jnp.float32)

    def one(i, carry):
        ref[0, i] = zero
        ref[9, i] = zero
        ref[i, 0] = zero
        ref[i, 9] = zero
        return carry

    lax.fori_loop(0, 10, one, 0)


def first_shares_kernel(n_gx, n_gy, b_hbm, kap_hbm, kxl_hbm, kxh_hbm, kyl_hbm, kyh_hbm, out_ref, *refs):
    h_ref, g_ref, gf_ref, rows_ref, b_ref, KX, KY, sems = refs
    copies = run_copies(
        [
            (kyl_hbm, KY.at[0]),
            (kap_hbm, KY.at[1]),
            (kyh_hbm, KY.at[2]),
            (kxl_hbm.at[7], KX.at[0]),
            (kxh_hbm.at[0], KX.at[1]),
            (b_hbm, b_ref),
        ],
        sems,
    )
    has_x, has_y = place(n_gx, n_gy)
    fill_border(h_ref)
    for copy in copies:
        copy.wait()

    def one_row(i, carry):
        g_ref[i] = OMEGA / (6.0 + KY[1, i])
        gf_ref[2, pl.ds(i, 1)] = OMEGA / (6.0 + KY[0, i, 7:8]) * has_y[0]
        gf_ref[3, pl.ds(i, 1)] = OMEGA / (6.0 + KY[2, i, 0:1]) * has_y[2]
        for j in range(8):
            put(h_ref, i + 1, j + 1, mul(row(g_ref, i, j), ld(b_ref, i, j)))
        return carry

    lax.fori_loop(0, 8, one_row, 0)
    gf_ref[0] = OMEGA / (6.0 + KX[0]) * has_x[0]
    gf_ref[1] = OMEGA / (6.0 + KX[1]) * has_x[2]
    out_ref[...] = shares(
        h_ref,
        lambda i, j: ld(b_ref, i, j),
        lambda i, j: row(g_ref, i, j),
        lambda f, n: row(gf_ref, f, n),
        rows_ref,
    )


def coarse_values(recv_ref, inv_ref, c_ref, count, valid):
    lane = lanes()
    r = lax.broadcasted_iota(jnp.int32, (8, L), 0)
    keep = (lane // 16) == r
    pieces = []
    for t in range(3):
        for j in range(count):
            value = None
            for dy in (-1, 0, 1):
                if not 0 <= j - dy < count:
                    continue
                for c in range(2):
                    term = recv_ref[c * count + j - dy, pl.ds(t * 3 + dy + 1, 1), :]
                    value = term if value is None else value + term
            pieces.append(jnp.where(keep, jnp.broadcast_to(value, (8, L)), 0.0))
    i0 = lax.broadcasted_iota(jnp.int32, (L, L), 0)
    i1 = lax.broadcasted_iota(jnp.int32, (L, L), 1)
    fold = jnp.where((i0 % 16) == (i1 % 16), 1.0, 0.0)
    spread = jnp.dot(
        jnp.concatenate(pieces, axis=0), fold, precision=HIGHEST, preferred_element_type=jnp.float32
    )
    for t in range(3):
        values = []
        for part in range(0, count, 8):
            out = jnp.zeros((8, L), jnp.float32)
            for j in range(part, min(part + 8, count)):
                at = (t * count + j) * 8
                out = jnp.where((lane // 16) == j - part, spread[at : at + 8], out)
            values.append(out)
        d = jnp.concatenate(values, axis=1)[:, : count * 16]
        c = lax.dot_general(
            d,
            inv_ref[t],
            (((1,), (1,)), ((), ())),
            precision=HIGHEST,
            preferred_element_type=jnp.float32,
        )
        for jj in range(3):
            for k in range(CH):
                out = jnp.zeros((8, L), jnp.float32)
                for q in range(4):
                    m = jj * 16 + k * 4 + q
                    out = jnp.where((lane // 32) == q, jnp.broadcast_to(c[:, m : m + 1], (8, L)), out)
                c_ref[t * 3 + jj, :, k * L : (k + 1) * L] = out * (valid[0][t] * valid[1][jj])


def place(n_gx, n_gy):
    gx = lax.axis_index("z") * 2 + lax.axis_index("core")
    gy = lax.axis_index("gy")

    def flag(condition):
        return jnp.where(condition, 1.0, 0.0).astype(jnp.float32)

    one = jnp.float32(1.0)
    return (flag(gx > 0), one, flag(gx < n_gx - 1)), (flag(gy > 0), one, flag(gy < n_gy - 1))


def run_copies(pairs, sems, base=0):
    copies = []
    for n, (src, dst) in enumerate(pairs):
        copy = pltpu.make_async_copy(src, dst, sems.at[base + n])
        copy.start()
        copies.append(copy)
    return copies


def pack_kernel(n_gy, cells, inverse, to_high, to_low, m_high, m_low, b_ref, inv_ref, in_sems, sems):
    gy = lax.axis_index("gy")
    inv = []
    for n in range(6):
        block = jnp.clip(gy - 1 + n // 2, 0, n_gy - 1) * 16 + (n % 2) * 8
        half = (n % 2) * 256
        inv.append(
            (inverse.at[pl.ds(pl.multiple_of(block, 8), 8)], inv_ref.at[n // 2, :, half : half + 256])
        )
    for copy in run_copies([(cells, b_ref)] + inv, in_sems):
        copy.wait()
    pairs = []
    for x in range(8):
        pairs.append((b_ref.at[8 * x + 4 : 8 * x + 8], to_high.at[x]))
        pairs.append((b_ref.at[8 * x : 8 * x + 4], to_low.at[x]))
    for start, m in ((32, m_high), (0, m_low)):
        pairs.append((b_ref.at[start : start + 32], m.at[0:CELLS]))
        pairs.append((inv_ref, m.at[INV_AT:LAST]))
    for copy in run_copies(pairs, sems):
        copy.wait()


def pass_kernel(*refs):
    pass


CELLS, LOW_AT, HIGH_AT, KAPPA_AT, INV_AT, LAST = 32, 32, 38, 44, 50, 53


def corner_segments():
    at = 0
    for a in (1, 2, 3):
        yield a, at, 4 - a
        at += 4 - a


def merge_kernel(first, n_z, n_gy, own_ref, low_ref, high_ref, y_low, y_high, m_high, m_low, *refs):
    if first:
        kyl, kyh = refs[:2]
        refs = refs[2:]
    out_ref, to_high, to_low, high_part, low_part, sems = refs
    pairs = []
    for up, m in ((True, high_part), (False, low_part)):
        for a, at, wide in corner_segments():
            x = 8 - a if up else a - 1
            pairs.append((y_low.at[x * 4 + 4 - wide : x * 4 + 4], m.at[at : at + wide]))
            pairs.append((y_high.at[x * 4 : x * 4 + wide], m.at[6 + at : 6 + at + wide]))
        if first:
            x = 5 if up else 0
            pairs.append((kyl.at[x : x + 3], m.at[12:15]))
            pairs.append((kyh.at[x : x + 3], m.at[15:18]))
    copies = run_copies(pairs, sems)
    z, core = lax.axis_index("z"), lax.axis_index("core")
    below = jnp.where(z > 0, 1.0, 0.0).astype(jnp.float32)
    above = jnp.where(z < n_z - 1, 1.0, 0.0).astype(jnp.float32)
    own = [own_ref[3 * t : 3 * t + 3] for t in range(3)]
    low = [low_ref[3 * t : 3 * t + 3] * below for t in range(3)]
    high = [high_ref[3 * t : 3 * t + 3] * above for t in range(3)]
    even = [own[0] + low[2], own[1], own[2] + high[0], high[1]]
    odd = [low[1], own[0] + low[2], own[1], own[2] + high[0]]
    slabs = [jnp.where(core == 0, e, o) for e, o in zip(even, odd)]
    for t in range(3):
        for n in range(n_gy):
            out_ref[n, 3 * t : 3 * t + 3] = slabs[t]
            out_ref[n_gy + n, 3 * t : 3 * t + 3] = slabs[t + 1]
    for copy in copies:
        copy.wait()
    end = INV_AT if first else KAPPA_AT
    for copy in run_copies([(high_part, to_high.at[CELLS:end]), (low_part, to_low.at[CELLS:end])], sems):
        copy.wait()


def cycle_kernel(first, n_gx, n_gy, *refs):
    f_own, f_yl, f_yh, f_xl, f_xh, b_xl, b_xh = refs[:7]
    kap_ref, kxl, kxh, kyl, kyh, recv_hbm, c_own = refs[7:14]
    refs = refs[14:]
    if first:
        z_out, q_out, dots_ref, out_ref = refs[:4]
        sends = refs[4:8]
        refs = refs[8:]
    else:
        extra_hbm, earlier_ref, z_out, q_out, dots_ref = refs[:5]
        refs = refs[5:]
    F, A, B, G, KC, KX, KY, inv_ref, c_ref, h_ref, gf_ref, rows_ref, z_ref, q_ref, recv_ref, extra_ref, sems = refs
    has_x, has_y = place(n_gx, n_gy)
    gy = lax.axis_index("gy")

    pairs = [(recv_hbm, recv_ref)]
    for jj in range(3):
        block = jnp.clip(gy - 1 + jj, 0, n_gy - 1)
        pairs.append(
            (c_own.at[pl.ds(pl.multiple_of(block * 16, 16), 16)], inv_ref.at[1, jj * 16 : jj * 16 + 16])
        )
    for t, ref in ((0, b_xl), (2, b_xh)):
        for n in range(6):
            half = (n % 2) * 256
            pairs.append((ref.at[INV_AT + n // 2, :, half : half + 256], inv_ref.at[t, n * 8 : n * 8 + 8]))
    n_inv = len(pairs)
    pairs += [
        (b_xl.at[KAPPA_AT : KAPPA_AT + 6], KC.at[0]),
        (b_xh.at[KAPPA_AT : KAPPA_AT + 6], KC.at[1]),
        (kap_ref, KY.at[1]),
        (kyl, KY.at[0]),
        (kyh, KY.at[2]),
        (kxl.at[4:8], KX.at[0]),
        (kxh.at[0:4], KX.at[1]),
    ]
    n_kappa = len(pairs)
    pairs += [
        (f_own, F.at[4:12, 4:12]),
        (f_yl, F.at[4:12, 0:4]),
        (f_yh, F.at[4:12, 12:16]),
    ]
    for low, ref in ((True, f_xl), (False, f_xh)):
        for i in range(4):
            pairs.append((ref.at[8 * i : 8 * i + 8], F.at[i if low else 12 + i, 4:12]))
        for a, at, wide in corner_segments():
            x = 4 - a if low else 11 + a
            pairs.append((ref.at[LOW_AT + at : LOW_AT + at + wide], F.at[x, 4 - wide : 4]))
            pairs.append((ref.at[HIGH_AT + at : HIGH_AT + at + wide], F.at[x, 12 : 12 + wide]))
    n_field = len(pairs)
    if not first:
        pairs.append((extra_hbm, extra_ref))
    copies = run_copies(pairs, sems)

    zero = jnp.zeros((8, CH * L), jnp.float32)
    for x, y in [(a, b) for a in range(4) for b in range(4) if (4 - a) + (4 - b) > 4]:
        for xx, yy in ((x, y), (x, 15 - y), (15 - x, y), (15 - x, 15 - y)):
            F[xx, yy] = zero

    def inv_diag(kappa):
        return OMEGA / (6.0 + kappa)

    for copy in copies[:n_inv]:
        copy.wait()
    coarse_values(recv_ref, inv_ref, c_ref, n_gy, (has_x, has_y))

    for copy in copies[n_inv:n_kappa]:
        copy.wait()
    for i in range(8):
        G[4 + i, 8:16] = inv_diag(KY[1, i])
        G[4 + i, 0:8] = inv_diag(KY[0, i]) * has_y[0]
        G[4 + i, 16:24] = inv_diag(KY[2, i]) * has_y[2]
    for a in range(4):
        G[a, 8:16] = inv_diag(KX[0, a]) * has_x[0]
        G[12 + a, 8:16] = inv_diag(KX[1, a]) * has_x[2]
    for side, sx in ((0, -1), (1, 1)):
        for half, sy in ((0, -1), (1, 1)):
            mask = has_x[1 + sx] * has_y[1 + sy]
            y = 0 if sy < 0 else 16
            G[0 if sx < 0 else 15, y : y + 8] = zero
            for i in range(3):
                G[1 + i if sx < 0 else 12 + i, y : y + 8] = inv_diag(KC[side, 3 * half + i]) * mask
    for copy in copies[n_kappa:n_field]:
        copy.wait()

    lane = lanes()

    def start_row(x, carry):
        for y in range(16):
            put(A, x, y, mul(row(G, x, y + 4), ld(F, x, y)))
        return carry

    lax.fori_loop(0, 16, start_row, 0)

    def sweep(src, dst, edge, coarse):
        def one_row(x, carry):
            t = jnp.where(x >= 4, 1, 0) + jnp.where(x >= 12, 1, 0)
            for y, here, near in beside_rows(src, x, edge, 16 - edge, lane):
                new = add(scale(THIRD, here), mul(add(ld(F, x, y), near), row(G, x, y + 4)))
                if coarse:
                    jj = (1 if y >= 4 else 0) + (1 if y >= 12 else 0)
                    new = add(new, [c_ref[t * 3 + jj, :, k * L : (k + 1) * L] for k in range(CH)])
                put(dst, x, y, new)
            return carry

        lax.fori_loop(edge, 16 - edge, one_row, 0, unroll=2)

    sweep(A, B, 1, True)
    sweep(B, A, 2, False)
    sweep(A, B, 3, False)
    for copy in copies[n_field:]:
        copy.wait()
    if first:
        fill_border(h_ref)
    nil = jnp.zeros((8, L), jnp.float32)

    def image_row(i, carry):
        fz, zq, ez = carry
        x = i + 4
        for y, here, near in beside_rows(B, x, 4, 12, lane):
            j = y - 4
            kappa = row(KY.at[1], i, j)
            image = [(6.0 + kappa[k]) * here[k] - near[k] for k in range(CH)]
            put(z_ref, i, j, here)
            put(q_ref, i, j, image)
            source = ld(F, x, y)
            fz = functools.reduce(lambda a, b: a + b, mul(source, here), fz)
            zq = functools.reduce(lambda a, b: a + b, mul(here, image), zq)
            if first:
                put(h_ref, i + 1, j + 1, mul(row(G, x, y + 4), image))
            else:
                ez = functools.reduce(lambda a, b: a + b, mul(ld(extra_ref, i, j), here), ez)
        return fz, zq, ez

    fz, zq, ez = lax.fori_loop(0, 8, image_row, (nil, nil, nil))
    if first:
        dots_ref[0] = fz
        dots_ref[1] = zq
        copies = run_copies(
            [
                (q_ref.at[0:8, 4:8], sends[0]),
                (q_ref.at[0:8, 0:4], sends[1]),
            ]
            + [(q_ref.at[4 + i], sends[2].at[8 * i : 8 * i + 8]) for i in range(4)]
            + [(q_ref.at[i], sends[3].at[8 * i : 8 * i + 8]) for i in range(4)]
            + [
                (q_ref, q_out),
                (z_ref, z_out),
            ],
            sems,
        )
        gf_ref[0] = G[3, 8:16]
        gf_ref[1] = G[12, 8:16]
        for i in range(8):
            gf_ref[2, pl.ds(i, 1)] = G[4 + i, 7:8]
            gf_ref[3, pl.ds(i, 1)] = G[4 + i, 16:17]
        out_ref[...] = shares(
            h_ref,
            lambda i, j: ld(q_ref, i, j),
            lambda i, j: row(G, i + 4, j + 8),
            lambda f, n: row(gf_ref, f, n),
            rows_ref,
        )
        for copy in copies:
            copy.wait()
    else:
        copies = run_copies([(z_ref, z_out), (q_ref, q_out)], sems)
        total = [earlier_ref[0], earlier_ref[1], fz, zq, ez]
        packed = nil
        for k, part in enumerate(total):
            packed = jnp.where(lane == k, jnp.sum(part, axis=1, keepdims=True), packed)
        for n in range(2 * n_gy):
            dots_ref[n] = packed
        for copy in copies:
            copy.wait()


def combine_kernel(sums_ref, *refs):
    sources, outs = refs[:5], refs[5:7]
    b_ref, z_ref, q_ref, w_ref, v_ref = refs[7:12]
    x_keep, r_keep, in_sems, sems = refs[12:]
    fetched = [
        run_copies(
            [(src.at[2 * i : 2 * i + 2], dst.at[2 * i : 2 * i + 2]) for src, dst in zip(sources, refs[7:12])],
            in_sems,
            5 * i,
        )
        for i in range(4)
    ]
    sums = sums_ref[0]
    for n in range(1, sums_ref.shape[0]):
        sums = sums + sums_ref[n]
    bz, zq, qw, wv, bw = (sums[:, k : k + 1] for k in range(5))
    a0 = bz / zq
    e1 = bz - a0 * (bw + zq) + a0 * a0 * qw
    beta = e1 / bz
    z1q = zq - a0 * qw
    z1v = zq - 2.0 * a0 * qw + a0 * a0 * wv
    a1 = e1 / (z1v + 2.0 * beta * z1q + beta * beta * zq)
    cz = jnp.broadcast_to(a0 + a1 * (1.0 + beta), (8, CH * L))
    cw = jnp.broadcast_to(a1 * a0, (8, CH * L))
    copies = []
    for n in range(4):
        for copy in fetched[n]:
            copy.wait()
        for i in (2 * n, 2 * n + 1):
            for j in range(8):
                x_keep[i, j] = cz * z_ref[i, j] - cw * w_ref[i, j]
                r_keep[i, j] = b_ref[i, j] - cz * q_ref[i, j] + cw * v_ref[i, j]
        part = slice(2 * n, 2 * n + 2)
        copies += run_copies([(x_keep.at[part], outs[0].at[part]), (r_keep.at[part], outs[1].at[part])], sems, 2 * n)
    for copy in copies:
        copy.wait()


def shift(value, axes, sizes, steps):
    pairs = []
    total = 1
    for n in sizes:
        total *= n
    for flat in range(total):
        rest, target = flat, 0
        weight = 1
        for n, step in zip(reversed(sizes), reversed(steps)):
            at = rest % n
            rest //= n
            target += ((at + step) % n) * weight
            weight *= n
        pairs.append((flat, target))
    return lax.ppermute(value, axes, pairs)


VM = pl.BlockSpec(memory_space=pltpu.VMEM)
HB = pl.BlockSpec(memory_space=pl.ANY)


def solution(mesh):
    n_gx, n_gy = mesh.shape["gx"], mesh.shape["gy"]
    n_z = n_gx // 2
    fine = Mesh(mesh.devices.reshape(n_z, 2, n_gy), ALL)

    f32 = jnp.float32

    def shape(*dims):
        return jax.ShapeDtypeStruct(dims, f32)

    tile = shape(8, 8, 8, CH * L)
    y_face = shape(8, 4, 8, CH * L)

    def along_gy(faces):
        return [shift(faces[0], ("gy",), (n_gy,), (1,)), shift(faces[1], ("gy",), (n_gy,), (-1,))]

    def exchange(own, faces, messages, more):
        low = shift(own, ("z",), (n_z,), (1,))
        high = shift(own, ("z",), (n_z,), (-1,))
        size = INV_AT if more else KAPPA_AT
        part = pltpu.VMEM((size - CELLS, 8, CH * L), f32)
        out, to_high, to_low = pl.pallas_call(
            functools.partial(merge_kernel, bool(more), n_z, n_gy),
            out_shape=[shape(2 * n_gy, 9, L)] + [shape(*m.shape) for m in messages],
            in_specs=[VM] * 3 + [HB] * (4 + len(more)),
            out_specs=[VM, HB, HB],
            input_output_aliases={5: 1, 6: 2},
            scratch_shapes=[part, part, pltpu.SemaphoreType.DMA((20,))],
            compiler_params=GRANT,
            name="merge_shares",
        )(own, low, high, *(f.reshape(32, 8, CH * L) for f in faces), *messages, *more)
        from_low = shift(to_high, GX, (n_gx,), (1,))
        from_high = shift(to_low, GX, (n_gx,), (-1,))
        return lax.all_to_all(out, SLAB2, 0, 0), [from_low, from_high]

    def body(b, kappa, inverse):
        around = [
            shift(kappa, GX, (n_gx,), (1,)),
            shift(kappa, GX, (n_gx,), (-1,)),
            shift(kappa, ("gy",), (n_gy,), (1,)),
            shift(kappa, ("gy",), (n_gy,), (-1,)),
        ]
        packed = pl.pallas_call(
            functools.partial(pack_kernel, n_gy),
            out_shape=[y_face, y_face] + [shape(LAST, 8, CH * L)] * 2,
            in_specs=[HB, HB],
            out_specs=[HB] * 4,
            scratch_shapes=[
                pltpu.VMEM((64, 8, CH * L), f32),
                pltpu.VMEM((3, 8, CH * L), f32),
                pltpu.SemaphoreType.DMA((7,)),
                pltpu.SemaphoreType.DMA((20,)),
            ],
            compiler_params=WHOLE,
            name="pack_faces",
        )(b.reshape(64, 8, CH * L), inverse)
        behind = pl.pallas_call(
            pass_kernel,
            out_shape=[y_face, y_face],
            in_specs=[HB] * 6,
            out_specs=[HB] * 2,
            input_output_aliases={4: 0, 5: 1},
            compiler_params=WHOLE,
            name="pass_faces",
        )(*around, packed[0], packed[1])
        b_faces = along_gy(behind)
        own = pl.pallas_call(
            functools.partial(first_shares_kernel, n_gx, n_gy),
            out_shape=shape(9, L),
            in_specs=[HB] * 6,
            out_specs=VM,
            scratch_shapes=[
                pltpu.VMEM((10, 10, 8, CH * L), f32),
                pltpu.VMEM((8, 8, CH * L), f32),
                pltpu.VMEM((4, 8, CH * L), f32),
                pltpu.VMEM((8, 8, CH * L), f32),
                pltpu.VMEM((8, 8, 8, CH * L), f32),
                pltpu.VMEM((2, 8, CH * L), f32),
                pltpu.VMEM((3, 8, 8, CH * L), f32),
                pltpu.SemaphoreType.DMA((6,)),
            ],
            compiler_params=GRANT,
            name="first_shares",
        )(b, kappa, *around)

        def cycle(first, field, faces, messages, b_messages, received, more):
            outs = [tile, tile]
            out_specs = [HB, HB, VM]
            if first:
                outs += [shape(2, 8, L), shape(9, L), y_face, y_face]
                outs += [shape(KAPPA_AT, 8, CH * L)] * 2
                out_specs += [VM, HB, HB, HB, HB]
            else:
                outs += [shape(2 * n_gy, 8, L)]
            big = pltpu.VMEM((16, 16, 8, CH * L), f32)
            own_tile = pltpu.VMEM((8, 8, 8, CH * L), f32)
            return pl.pallas_call(
                functools.partial(cycle_kernel, first, n_gx, n_gy),
                out_shape=outs,
                in_specs=[HB] * 14 + ([HB, VM] if more else []),
                out_specs=out_specs,
                scratch_shapes=[
                    big,
                    big,
                    big,
                    pltpu.VMEM((16, 24, CH * L), f32),
                    pltpu.VMEM((2, 6, 8, CH * L), f32),
                    pltpu.VMEM((2, 4, 8, CH * L), f32),
                    pltpu.VMEM((3, 8, 8, CH * L), f32),
                    pltpu.VMEM((3, 48, 16 * n_gy), f32),
                    pltpu.VMEM((9, 8, CH * L), f32),
                    pltpu.VMEM((10, 10, 8, CH * L), f32),
                    pltpu.VMEM((4, 8, CH * L), f32),
                    pltpu.VMEM((8, 8, CH * L), f32),
                    own_tile,
                    own_tile,
                    pltpu.VMEM((2 * n_gy, 9, L), f32),
                    own_tile,
                    pltpu.SemaphoreType.DMA((52,)),
                ],
                compiler_params=GRANT,
                name="first_cycle" if first else "second_cycle",
            )(field, *faces, *messages, *b_messages, kappa, *around, received, inverse, *more)

        received, b_messages = exchange(own, b_faces, packed[2:], around[2:])
        z0, q0, dots, own, *sends = cycle(True, b, b_faces, b_messages, b_messages, received, [])
        q_faces = along_gy(sends[:2])
        received, messages = exchange(own, q_faces, sends[2:], [])
        w0, v0, packed = cycle(False, q0, q_faces, messages, b_messages, received, [b, dots])

        near_sum = jnp.sum(lax.all_to_all(packed, SLAB2, 0, 0), axis=0)
        sums = lax.all_to_all(jnp.broadcast_to(near_sum, (n_z, 8, L)), "z", 0, 0)
        return pl.pallas_call(
            combine_kernel,
            out_shape=[tile, tile],
            in_specs=[VM] + [HB] * 5,
            out_specs=[HB, HB],
            scratch_shapes=[pltpu.VMEM((8, 8, 8, CH * L), f32)] * 7
            + [pltpu.SemaphoreType.DMA((20,)), pltpu.SemaphoreType.DMA((8,))],
            compiler_params=GRANT,
            name="combine",
        )(sums, b, z0, q0, w0, v0)

    field = P(GX, "gy", None, None)
    return jax.shard_map(
        body,
        mesh=fine,
        in_specs=(field, P(GX, "gy", None), P(GX, None)),
        out_specs=(field, field),
        check_vma=False,
    )
```

```python
import functools

import jax
import jax.numpy as jnp
from jax import lax
from jax.experimental import pallas as pl
from jax.experimental.pallas import tpu as pltpu
from jax.sharding import Mesh
from jax.sharding import PartitionSpec as P

OMEGA = 2.0 / 3.0
THIRD = 1.0 / 3.0
L = 128
CH = 4
HALO = 4
GX = ("z", "core")
SLAB2 = ("core", "gy")
ALL = ("z", "core", "gy")
HIGHEST = lax.Precision.HIGHEST
WHOLE = pltpu.CompilerParams(vmem_limit_bytes=(64 << 20) - (64 << 10))
GRANT = pltpu.CompilerParams(vmem_limit_bytes=(63 << 20) + (256 << 10))


def lanes():
    return lax.broadcasted_iota(jnp.int32, (8, L), 1)


def ld(ref, x, y):
    return [ref[x, y, :, k * L : (k + 1) * L] for k in range(CH)]


def row(ref, x, y):
    return [jnp.broadcast_to(ref[x, pl.ds(y, 1), k * L : (k + 1) * L], (8, L)) for k in range(CH)]


def put(ref, x, y, values):
    for k in range(CH):
        ref[x, y, :, k * L : (k + 1) * L] = values[k]


def zsum(v, lane):
    up = [pltpu.roll(c, 1, 1) for c in v]
    down = [pltpu.roll(c, L - 1, 1) for c in v]
    out = []
    for k in range(CH):
        before = up[k - 1] if k > 0 else jnp.zeros_like(up[0])
        after = down[k + 1] if k < CH - 1 else jnp.zeros_like(up[0])
        out.append(jnp.where(lane == 0, before, up[k]) + jnp.where(lane == L - 1, after, down[k]))
    return out


def add(*terms):
    return [functools.reduce(lambda a, b: a + b, t) for t in zip(*terms)]


def mul(a, b):
    return [p * q for p, q in zip(a, b)]


def scale(s, a):
    return [s * p for p in a]


def join(v):
    return jnp.concatenate(v, axis=1)


def beside_rows(ref, x, lo, hi, lane):
    prev, here = ld(ref, x, lo - 1), ld(ref, x, lo)
    for y in range(lo, hi):
        after = ld(ref, x, y + 1)
        near = add(prev, after, ld(ref, x - 1, y), ld(ref, x + 1, y), zsum(here, lane))
        yield y, here, near
        prev, here = here, after


def shares(h_ref, source, g_own, g_faces, rows_ref):
    lane = lanes()
    zero = [jnp.zeros((8, L), jnp.float32)] * CH

    def one_row(i, carry):
        a1, ylo, yhi = carry
        total = zero
        for y, here, near in beside_rows(h_ref, i + 1, 1, 9, lane):
            j = y - 1
            t1 = add(scale(THIRD, source(i, j)), near)
            s = mul(g_own(i, j), t1)
            a1 = add(a1, t1)
            total = add(total, s)
            if j == 0:
                ylo = add(ylo, s)
            if j == 7:
                yhi = add(yhi, s)
        for k in range(CH):
            rows_ref[i, :, k * L : (k + 1) * L] = total[k]
        return a1, ylo, yhi

    a1, ylo, yhi = lax.fori_loop(0, 8, one_row, (zero, zero, zero))
    rows = [[rows_ref[i, :, k * L : (k + 1) * L] for k in range(CH)] for i in range(8)]
    s_all = add(*rows)
    edges = (rows[0], rows[7], ylo, yhi)
    faces = []
    for f, (cells, edge) in enumerate(
        zip(
            (
                [(1, j + 1) for j in range(8)],
                [(8, j + 1) for j in range(8)],
                [(i + 1, 1) for i in range(8)],
                [(i + 1, 8) for i in range(8)],
            ),
            edges,
        )
    ):
        t_sum, s_sum = zero, zero
        for n, (x, y) in enumerate(cells):
            t = ld(h_ref, x, y)
            s = mul(g_faces(f, n), t)
            t_sum, s_sum = add(t_sum, t), add(s_sum, s)
            if n == 0:
                first = s
            if n == 7:
                last = s
        part = add(
            scale(THIRD, t_sum),
            edge,
            scale(3.0, s_sum),
            scale(-1.0, add(first, last)),
            zsum(s_sum, lane),
        )
        faces.append((part, s_sum, first, last))
    (xl, sxl, xl0, xl7), (xh, sxh, xh0, xh7), (yl, syl, yl0, yl7), (yh, syh, yh0, yh7) = faces
    own = add(
        scale(THIRD, a1),
        scale(4.0, s_all),
        scale(-1.0, add(*edges)),
        sxl,
        sxh,
        syl,
        syh,
        zsum(s_all, lane),
    )
    parts = [
        add(xl0, yl0),
        xl,
        add(xl7, yh0),
        yl,
        own,
        yh,
        add(xh0, yl7),
        xh,
        add(xh7, yh7),
    ]
    stacked = jnp.concatenate([join(p) for p in parts], axis=0)
    zi = lax.broadcasted_iota(jnp.int32, (CH * L, L), 0)
    li = lax.broadcasted_iota(jnp.int32, (CH * L, L), 1)
    fold = jnp.where((zi // 32) == (li % 16), 1.0 / 2048.0, 0.0)
    sums = jnp.dot(stacked, fold, precision=HIGHEST, preferred_element_type=jnp.float32)
    r = lax.broadcasted_iota(jnp.int32, (8, L), 0)
    keep = (lane // 16) == r
    out = [
        jnp.sum(jnp.where(keep, sums[8 * n : 8 * n + 8], 0.0), axis=0, keepdims=True)
        for n in range(9)
    ]
    return jnp.concatenate(out, axis=0)


def fill_border(ref):
    zero = jnp.zeros((8, CH * L), jnp.float32)

    def one(i, carry):
        ref[0, i] = zero
        ref[9, i] = zero
        ref[i, 0] = zero
        ref[i, 9] = zero
        return carry

    lax.fori_loop(0, 10, one, 0)


def first_shares_kernel(n_gx, n_gy, b_hbm, kap_hbm, kxl_hbm, kxh_hbm, kyl_hbm, kyh_hbm, out_ref, *refs):
    h_ref, g_ref, gf_ref, rows_ref, b_ref, KX, KY, sems = refs
    copies = run_copies(
        [
            (kyl_hbm, KY.at[0]),
            (kap_hbm, KY.at[1]),
            (kyh_hbm, KY.at[2]),
            (kxl_hbm.at[7], KX.at[0]),
            (kxh_hbm.at[0], KX.at[1]),
        ]
        + [(b_hbm.at[2 * i : 2 * i + 2], b_ref.at[2 * i : 2 * i + 2]) for i in range(4)],
        sems,
    )
    has_x, has_y = place(n_gx, n_gy)
    fill_border(h_ref)
    for copy in copies[:5]:
        copy.wait()

    def one_row(i, carry):
        g_ref[i] = OMEGA / (6.0 + KY[1, i])
        gf_ref[2, pl.ds(i, 1)] = OMEGA / (6.0 + KY[0, i, 7:8]) * has_y[0]
        gf_ref[3, pl.ds(i, 1)] = OMEGA / (6.0 + KY[2, i, 0:1]) * has_y[2]
        for j in range(8):
            put(h_ref, i + 1, j + 1, mul(row(g_ref, i, j), ld(b_ref, i, j)))
        return carry

    for n in range(4):
        copies[5 + n].wait()
        lax.fori_loop(2 * n, 2 * n + 2, one_row, 0)
    gf_ref[0] = OMEGA / (6.0 + KX[0]) * has_x[0]
    gf_ref[1] = OMEGA / (6.0 + KX[1]) * has_x[2]
    out_ref[...] = shares(
        h_ref,
        lambda i, j: ld(b_ref, i, j),
        lambda i, j: row(g_ref, i, j),
        lambda f, n: row(gf_ref, f, n),
        rows_ref,
    )


def coarse_values(recv_ref, inv_ref, c_ref, count, valid):
    lane = lanes()
    r = lax.broadcasted_iota(jnp.int32, (8, L), 0)
    keep = (lane // 16) == r
    pieces = []
    for t in range(3):
        for j in range(count):
            value = None
            for dy in (-1, 0, 1):
                if not 0 <= j - dy < count:
                    continue
                for c in range(2):
                    term = recv_ref[c * count + j - dy, t * 3 + dy + 1]
                    value = term if value is None else value + term
            pieces.append(jnp.where(keep, jnp.broadcast_to(value, (8, L)), 0.0))
    i0 = lax.broadcasted_iota(jnp.int32, (L, L), 0)
    i1 = lax.broadcasted_iota(jnp.int32, (L, L), 1)
    fold = jnp.where((i0 % 16) == (i1 % 16), 1.0, 0.0)
    spread = jnp.dot(
        jnp.concatenate(pieces, axis=0), fold, precision=HIGHEST, preferred_element_type=jnp.float32
    )
    for t in range(3):
        values = []
        for part in range(0, count, 8):
            out = jnp.zeros((8, L), jnp.float32)
            for j in range(part, min(part + 8, count)):
                at = (t * count + j) * 8
                out = jnp.where((lane // 16) == j - part, spread[at : at + 8], out)
            values.append(out)
        d = jnp.concatenate(values, axis=1)[:, : count * 16]
        c = lax.dot_general(
            d,
            inv_ref[t],
            (((1,), (1,)), ((), ())),
            precision=HIGHEST,
            preferred_element_type=jnp.float32,
        )
        for jj in range(3):
            for k in range(CH):
                out = jnp.zeros((8, L), jnp.float32)
                for q in range(4):
                    m = jj * 16 + k * 4 + q
                    out = jnp.where((lane // 32) == q, jnp.broadcast_to(c[:, m : m + 1], (8, L)), out)
                c_ref[t * 3 + jj, :, k * L : (k + 1) * L] = out * (valid[0][t] * valid[1][jj])


def place(n_gx, n_gy):
    gx = lax.axis_index("z") * 2 + lax.axis_index("core")
    gy = lax.axis_index("gy")

    def flag(condition):
        return jnp.where(condition, 1.0, 0.0).astype(jnp.float32)

    one = jnp.float32(1.0)
    return (flag(gx > 0), one, flag(gx < n_gx - 1)), (flag(gy > 0), one, flag(gy < n_gy - 1))


def run_copies(pairs, sems, base=0):
    copies = []
    for n, (src, dst) in enumerate(pairs):
        copy = pltpu.make_async_copy(src, dst, sems.at[base + n])
        copy.start()
        copies.append(copy)
    return copies


def pack_kernel(n_gy, cells, inverse, to_high, to_low, m_high, m_low, b_ref, inv_ref, in_sems, sems):
    gy = lax.axis_index("gy")
    inv = []
    for n in range(6):
        block = jnp.clip(gy - 1 + n // 2, 0, n_gy - 1) * 16 + (n % 2) * 8
        half = (n % 2) * 256
        inv.append(
            (inverse.at[pl.ds(pl.multiple_of(block, 8), 8)], inv_ref.at[n // 2, :, half : half + 256])
        )
    for copy in run_copies([(cells, b_ref)] + inv, in_sems):
        copy.wait()
    pairs = []
    for x in range(8):
        pairs.append((b_ref.at[8 * x + 4 : 8 * x + 8], to_high.at[x]))
        pairs.append((b_ref.at[8 * x : 8 * x + 4], to_low.at[x]))
    for start, m in ((32, m_high), (0, m_low)):
        pairs.append((b_ref.at[start : start + 32], m.at[0:CELLS]))
        pairs.append((inv_ref, m.at[INV_AT:LAST]))
    for copy in run_copies(pairs, sems):
        copy.wait()


def pass_kernel(*refs):
    pass


CELLS, INV_AT, LAST = 32, 32, 35
HIGH_AT, KAPPA_AT, CORNERS = 6, 12, 18


def corner_segments():
    at = 0
    for a in (1, 2, 3):
        yield a, at, 4 - a
        at += 4 - a


def merge_kernel(first, n_z, n_gy, own_ref, low_ref, high_ref, y_low, y_high, *refs):
    if first:
        kyl, kyh = refs[:2]
        refs = refs[2:]
    out_ref, to_high, to_low, high_part, low_part, sems = refs
    pairs = []
    for up, m in ((True, high_part), (False, low_part)):
        for a, at, wide in corner_segments():
            x = 8 - a if up else a - 1
            pairs.append((y_low.at[x * 4 + 4 - wide : x * 4 + 4], m.at[at : at + wide]))
            pairs.append((y_high.at[x * 4 : x * 4 + wide], m.at[HIGH_AT + at : HIGH_AT + at + wide]))
        if first:
            x = 5 if up else 0
            pairs.append((kyl.at[x : x + 3], m.at[KAPPA_AT : KAPPA_AT + 3]))
            pairs.append((kyh.at[x : x + 3], m.at[KAPPA_AT + 3 : KAPPA_AT + 6]))
    copies = run_copies(pairs, sems)
    z, core = lax.axis_index("z"), lax.axis_index("core")
    below = jnp.where(z > 0, 1.0, 0.0).astype(jnp.float32)
    above = jnp.where(z < n_z - 1, 1.0, 0.0).astype(jnp.float32)
    own = [own_ref[n : n + 1] for n in range(9)]
    low = [low_ref[n : n + 1] * below for n in range(9)]
    high = [high_ref[n : n + 1] * above for n in range(9)]
    slabs = []
    for dy in range(3):
        even = [own[dy] + low[6 + dy], own[3 + dy], own[6 + dy] + high[dy], high[3 + dy]]
        odd = [low[3 + dy], own[dy] + low[6 + dy], own[3 + dy], own[6 + dy] + high[dy]]
        slabs.append([jnp.where(core == 0, e, o) for e, o in zip(even, odd)])
    for t in range(3):
        for dy in range(3):
            for n in range(n_gy):
                out_ref[n, 3 * t + dy] = slabs[dy][t]
                out_ref[n_gy + n, 3 * t + dy] = slabs[dy][t + 1]
    for copy in copies:
        copy.wait()
    for copy in run_copies([(high_part, to_high), (low_part, to_low)], sems):
        copy.wait()


def cycle_kernel(first, n_gx, n_gy, *refs):
    f_own, f_yl, f_yh, f_xl, f_xh, f_cl, f_ch, b_xl, b_xh, b_cl, b_ch = refs[:11]
    kap_ref, kxl, kxh, kyl, kyh, recv_hbm, c_own = refs[11:18]
    refs = refs[18:]
    if first:
        z_out, q_out, dots_ref, out_ref = refs[:4]
        sends = refs[4:8]
        refs = refs[8:]
    else:
        extra_hbm, earlier_ref, z_out, q_out, dots_ref = refs[:5]
        refs = refs[5:]
    F, A, B, G, KC, KX, KY, inv_ref, c_ref, h_ref, gf_ref, rows_ref, z_ref, q_ref, recv_ref, extra_ref, sems = refs
    has_x, has_y = place(n_gx, n_gy)
    gy = lax.axis_index("gy")

    pairs = [(recv_hbm, recv_ref)]
    for jj in range(3):
        block = jnp.clip(gy - 1 + jj, 0, n_gy - 1)
        pairs.append(
            (c_own.at[pl.ds(pl.multiple_of(block * 16, 16), 16)], inv_ref.at[1, jj * 16 : jj * 16 + 16])
        )
    for t, ref in ((0, b_xl), (2, b_xh)):
        for n in range(6):
            half = (n % 2) * 256
            pairs.append((ref.at[INV_AT + n // 2, :, half : half + 256], inv_ref.at[t, n * 8 : n * 8 + 8]))
    n_inv = len(pairs)
    pairs += [
        (b_cl.at[KAPPA_AT:CORNERS], KC.at[0]),
        (b_ch.at[KAPPA_AT:CORNERS], KC.at[1]),
        (kap_ref, KY.at[1]),
        (kyl, KY.at[0]),
        (kyh, KY.at[2]),
        (kxl.at[4:8], KX.at[0]),
        (kxh.at[0:4], KX.at[1]),
    ]
    n_kappa = len(pairs)
    pairs += [
        (f_own, F.at[4:12, 4:12]),
        (f_yl, F.at[4:12, 0:4]),
        (f_yh, F.at[4:12, 12:16]),
    ]
    for low, ref, corner in ((True, f_xl, f_cl), (False, f_xh, f_ch)):
        for i in range(4):
            pairs.append((ref.at[8 * i : 8 * i + 8], F.at[i if low else 12 + i, 4:12]))
        for a, at, wide in corner_segments():
            x = 4 - a if low else 11 + a
            pairs.append((corner.at[at : at + wide], F.at[x, 4 - wide : 4]))
            pairs.append((corner.at[HIGH_AT + at : HIGH_AT + at + wide], F.at[x, 12 : 12 + wide]))
    n_field = len(pairs)
    if not first:
        pairs.append((extra_hbm, extra_ref))
    copies = run_copies(pairs, sems)

    zero = jnp.zeros((8, CH * L), jnp.float32)
    for x, y in [(a, b) for a in range(4) for b in range(4) if (4 - a) + (4 - b) > 4]:
        for xx, yy in ((x, y), (x, 15 - y), (15 - x, y), (15 - x, 15 - y)):
            F[xx, yy] = zero

    def inv_diag(kappa):
        return OMEGA / (6.0 + kappa)

    for copy in copies[:n_inv]:
        copy.wait()
    coarse_values(recv_ref, inv_ref, c_ref, n_gy, (has_x, has_y))

    for copy in copies[n_inv:n_kappa]:
        copy.wait()
    for i in range(8):
        G[4 + i, 8:16] = inv_diag(KY[1, i])
        G[4 + i, 0:8] = inv_diag(KY[0, i]) * has_y[0]
        G[4 + i, 16:24] = inv_diag(KY[2, i]) * has_y[2]
    for a in range(4):
        G[a, 8:16] = inv_diag(KX[0, a]) * has_x[0]
        G[12 + a, 8:16] = inv_diag(KX[1, a]) * has_x[2]
    for side, sx in ((0, -1), (1, 1)):
        for half, sy in ((0, -1), (1, 1)):
            mask = has_x[1 + sx] * has_y[1 + sy]
            y = 0 if sy < 0 else 16
            G[0 if sx < 0 else 15, y : y + 8] = zero
            for i in range(3):
                G[1 + i if sx < 0 else 12 + i, y : y + 8] = inv_diag(KC[side, 3 * half + i]) * mask
    for copy in copies[n_kappa:n_field]:
        copy.wait()

    lane = lanes()

    def start_row(x, carry):
        for y in range(16):
            put(A, x, y, mul(row(G, x, y + 4), ld(F, x, y)))
        return carry

    lax.fori_loop(0, 16, start_row, 0)

    def sweep(src, dst, width, coarse):
        def one_row(x, reach):
            t = jnp.where(x >= 4, 1, 0) + jnp.where(x >= 12, 1, 0)
            for y, here, near in beside_rows(src, x, 4 - reach, 12 + reach, lane):
                new = add(scale(THIRD, here), mul(add(ld(F, x, y), near), row(G, x, y + 4)))
                if coarse:
                    jj = (1 if y >= 4 else 0) + (1 if y >= 12 else 0)
                    new = add(new, [c_ref[t * 3 + jj, :, k * L : (k + 1) * L] for k in range(CH)])
                put(dst, x, y, new)

        def inner(x, carry):
            one_row(x, width)
            return carry

        for a in range(1, width + 1):
            one_row(4 - a, width - a)
            one_row(11 + a, width - a)
        lax.fori_loop(4, 12, inner, 0, unroll=2)

    sweep(A, B, 3, True)
    sweep(B, A, 2, False)
    sweep(A, B, 1, False)
    for copy in copies[n_field:]:
        copy.wait()
    if first:
        fill_border(h_ref)
    nil = jnp.zeros((8, L), jnp.float32)

    def image_row(i, carry):
        fz, zq, ez = carry
        x = i + 4
        for y, here, near in beside_rows(B, x, 4, 12, lane):
            j = y - 4
            kappa = row(KY.at[1], i, j)
            image = [(6.0 + kappa[k]) * here[k] - near[k] for k in range(CH)]
            put(z_ref, i, j, here)
            put(q_ref, i, j, image)
            source = ld(F, x, y)
            fz = functools.reduce(lambda a, b: a + b, mul(source, here), fz)
            zq = functools.reduce(lambda a, b: a + b, mul(here, image), zq)
            if first:
                put(h_ref, i + 1, j + 1, mul(row(G, x, y + 4), image))
            else:
                ez = functools.reduce(lambda a, b: a + b, mul(ld(extra_ref, i, j), here), ez)
        return fz, zq, ez

    fz, zq, ez = lax.fori_loop(0, 8, image_row, (nil, nil, nil))
    if first:
        dots_ref[0] = fz
        dots_ref[1] = zq
        copies = run_copies(
            [
                (q_ref.at[0:8, 4:8], sends[0]),
                (q_ref.at[0:8, 0:4], sends[1]),
            ]
            + [(q_ref.at[4 + i], sends[2].at[8 * i : 8 * i + 8]) for i in range(4)]
            + [(q_ref.at[i], sends[3].at[8 * i : 8 * i + 8]) for i in range(4)]
            + [
                (q_ref, q_out),
                (z_ref, z_out),
            ],
            sems,
        )
        gf_ref[0] = G[3, 8:16]
        gf_ref[1] = G[12, 8:16]
        for i in range(8):
            gf_ref[2, pl.ds(i, 1)] = G[4 + i, 7:8]
            gf_ref[3, pl.ds(i, 1)] = G[4 + i, 16:17]
        out_ref[...] = shares(
            h_ref,
            lambda i, j: ld(q_ref, i, j),
            lambda i, j: row(G, i + 4, j + 8),
            lambda f, n: row(gf_ref, f, n),
            rows_ref,
        )
        for copy in copies:
            copy.wait()
    else:
        copies = run_copies([(z_ref, z_out), (q_ref, q_out)], sems)
        total = [earlier_ref[0], earlier_ref[1], fz, zq, ez]
        packed = nil
        sub = lax.broadcasted_iota(jnp.int32, (8, L), 0)
        for k, part in enumerate(total):
            packed = jnp.where(lane == 8 * k + sub, jnp.sum(part, axis=1, keepdims=True), packed)
        packed = jnp.sum(packed, axis=0, keepdims=True)
        for n in range(2 * n_gy):
            dots_ref[n] = packed
        for copy in copies:
            copy.wait()


def combine_kernel(sums_ref, *refs):
    sources, outs = refs[:5], refs[5:7]
    b_ref, z_ref, q_ref, w_ref, v_ref = refs[7:12]
    x_keep, r_keep, in_sems, sems = refs[12:]
    fetched = [
        run_copies(
            [(src.at[2 * i : 2 * i + 2], dst.at[2 * i : 2 * i + 2]) for src, dst in zip(sources, refs[7:12])],
            in_sems,
            5 * i,
        )
        for i in range(4)
    ]
    sums = sums_ref[0]
    for n in range(1, sums_ref.shape[0]):
        sums = sums + sums_ref[n]
    sums = jnp.broadcast_to(sums, (8, L))
    sub = lax.broadcasted_iota(jnp.int32, (8, L), 0)
    bz, zq, qw, wv, bw = (
        jnp.sum(jnp.where(lanes() == 8 * k + sub, sums, 0.0), axis=1, keepdims=True) for k in range(5)
    )
    a0 = bz / zq
    e1 = bz - a0 * (bw + zq) + a0 * a0 * qw
    beta = e1 / bz
    z1q = zq - a0 * qw
    z1v = zq - 2.0 * a0 * qw + a0 * a0 * wv
    a1 = e1 / (z1v + 2.0 * beta * z1q + beta * beta * zq)
    cz = jnp.broadcast_to(a0 + a1 * (1.0 + beta), (8, CH * L))
    cw = jnp.broadcast_to(a1 * a0, (8, CH * L))
    copies = []
    for n in range(4):
        for copy in fetched[n]:
            copy.wait()
        for i in (2 * n, 2 * n + 1):
            for j in range(8):
                x_keep[i, j] = cz * z_ref[i, j] - cw * w_ref[i, j]
                r_keep[i, j] = b_ref[i, j] - cz * q_ref[i, j] + cw * v_ref[i, j]
        part = slice(2 * n, 2 * n + 2)
        copies += run_copies([(x_keep.at[part], outs[0].at[part]), (r_keep.at[part], outs[1].at[part])], sems, 2 * n)
    for copy in copies:
        copy.wait()


def shift(value, axes, sizes, steps):
    pairs = []
    total = 1
    for n in sizes:
        total *= n
    for flat in range(total):
        rest, target = flat, 0
        weight = 1
        for n, step in zip(reversed(sizes), reversed(steps)):
            at = rest % n
            rest //= n
            target += ((at + step) % n) * weight
            weight *= n
        pairs.append((flat, target))
    return lax.ppermute(value, axes, pairs)


VM = pl.BlockSpec(memory_space=pltpu.VMEM)
HB = pl.BlockSpec(memory_space=pl.ANY)


def solution(mesh):
    n_gx, n_gy = mesh.shape["gx"], mesh.shape["gy"]
    n_z = n_gx // 2
    fine = Mesh(mesh.devices.reshape(n_z, 2, n_gy), ALL)

    f32 = jnp.float32

    def shape(*dims):
        return jax.ShapeDtypeStruct(dims, f32)

    tile = shape(8, 8, 8, CH * L)
    y_face = shape(8, 4, 8, CH * L)

    def along_gy(faces):
        return [shift(faces[0], ("gy",), (n_gy,), (1,)), shift(faces[1], ("gy",), (n_gy,), (-1,))]

    def after(first, then):
        return pl.pallas_call(
            pass_kernel,
            out_shape=[shape(*v.shape) for v in then],
            in_specs=[HB] * (len(first) + len(then)),
            out_specs=[HB] * len(then),
            input_output_aliases={len(first) + n: n for n in range(len(then))},
            compiler_params=WHOLE,
            name="pass_on",
        )(*first, *then)

    def along_gx(to_high, to_low):
        return [shift(to_high, GX, (n_gx,), (1,)), shift(to_low, GX, (n_gx,), (-1,))]

    def exchange(own, faces, messages, more):
        low = shift(own, ("z",), (n_z,), (1,))
        high = shift(own, ("z",), (n_z,), (-1,))
        cells = along_gx(*after((low, high), messages))
        size = CORNERS if more else KAPPA_AT
        part = pltpu.VMEM((size, 8, CH * L), f32)
        out, to_high, to_low = pl.pallas_call(
            functools.partial(merge_kernel, bool(more), n_z, n_gy),
            out_shape=[shape(2 * n_gy, 9, 1, L)] + [shape(size, 8, CH * L)] * 2,
            in_specs=[VM] * 3 + [HB] * (2 + len(more)),
            out_specs=[VM, HB, HB],
            scratch_shapes=[part, part, pltpu.SemaphoreType.DMA((20,))],
            compiler_params=GRANT,
            name="merge_shares",
        )(own, low, high, *(f.reshape(32, 8, CH * L) for f in faces), *more)
        corners = along_gx(to_high, to_low)
        return lax.all_to_all(out, SLAB2, 0, 0), cells + corners

    def body(b, kappa, inverse):
        around = [
            shift(kappa, GX, (n_gx,), (1,)),
            shift(kappa, GX, (n_gx,), (-1,)),
            shift(kappa, ("gy",), (n_gy,), (1,)),
            shift(kappa, ("gy",), (n_gy,), (-1,)),
        ]
        packed = pl.pallas_call(
            functools.partial(pack_kernel, n_gy),
            out_shape=[y_face, y_face] + [shape(LAST, 8, CH * L)] * 2,
            in_specs=[HB, HB],
            out_specs=[HB] * 4,
            scratch_shapes=[
                pltpu.VMEM((64, 8, CH * L), f32),
                pltpu.VMEM((3, 8, CH * L), f32),
                pltpu.SemaphoreType.DMA((7,)),
                pltpu.SemaphoreType.DMA((20,)),
            ],
            compiler_params=WHOLE,
            name="pack_faces",
        )(b.reshape(64, 8, CH * L), inverse)
        behind = after(around, packed[:2])
        b_faces = along_gy(behind)
        own = pl.pallas_call(
            functools.partial(first_shares_kernel, n_gx, n_gy),
            out_shape=shape(9, L),
            in_specs=[HB] * 6,
            out_specs=VM,
            scratch_shapes=[
                pltpu.VMEM((10, 10, 8, CH * L), f32),
                pltpu.VMEM((8, 8, CH * L), f32),
                pltpu.VMEM((4, 8, CH * L), f32),
                pltpu.VMEM((8, 8, CH * L), f32),
                pltpu.VMEM((8, 8, 8, CH * L), f32),
                pltpu.VMEM((2, 8, CH * L), f32),
                pltpu.VMEM((3, 8, 8, CH * L), f32),
                pltpu.SemaphoreType.DMA((9,)),
            ],
            compiler_params=GRANT,
            name="first_shares",
        )(b, kappa, *around)

        def cycle(first, field, faces, messages, b_messages, received, more):
            outs = [tile, tile]
            out_specs = [HB, HB, VM]
            if first:
                outs += [shape(2, 8, L), shape(9, L), y_face, y_face]
                outs += [shape(CELLS, 8, CH * L)] * 2
                out_specs += [VM, HB, HB, HB, HB]
            else:
                outs += [shape(2 * n_gy, 1, L)]
            big = pltpu.VMEM((16, 16, 8, CH * L), f32)
            own_tile = pltpu.VMEM((8, 8, 8, CH * L), f32)
            return pl.pallas_call(
                functools.partial(cycle_kernel, first, n_gx, n_gy),
                out_shape=outs,
                in_specs=[HB] * 18 + ([HB, VM] if more else []),
                out_specs=out_specs,
                scratch_shapes=[
                    big,
                    big,
                    big,
                    pltpu.VMEM((16, 24, CH * L), f32),
                    pltpu.VMEM((2, 6, 8, CH * L), f32),
                    pltpu.VMEM((2, 4, 8, CH * L), f32),
                    pltpu.VMEM((3, 8, 8, CH * L), f32),
                    pltpu.VMEM((3, 48, 16 * n_gy), f32),
                    pltpu.VMEM((9, 8, CH * L), f32),
                    pltpu.VMEM((10, 10, 8, CH * L), f32),
                    pltpu.VMEM((4, 8, CH * L), f32),
                    pltpu.VMEM((8, 8, CH * L), f32),
                    own_tile,
                    own_tile,
                    pltpu.VMEM((2 * n_gy, 9, 1, L), f32),
                    own_tile,
                    pltpu.SemaphoreType.DMA((52,)),
                ],
                compiler_params=GRANT,
                name="first_cycle" if first else "second_cycle",
            )(field, *faces, *messages, *b_messages, kappa, *around, received, inverse, *more)

        received, b_messages = exchange(own, b_faces, packed[2:], around[2:])
        z0, q0, dots, own, *sends = cycle(True, b, b_faces, b_messages, b_messages, received, [])
        q_faces = along_gy(sends[:2])
        received, messages = exchange(own, q_faces, sends[2:], [])
        w0, v0, packed = cycle(False, q0, q_faces, messages, b_messages, received, [b, dots])

        near_sum = jnp.sum(lax.all_to_all(packed, SLAB2, 0, 0), axis=0)
        sums = lax.all_to_all(jnp.broadcast_to(near_sum, (n_z, 1, L)), "z", 0, 0)
        return pl.pallas_call(
            combine_kernel,
            out_shape=[tile, tile],
            in_specs=[VM] + [HB] * 5,
            out_specs=[HB, HB],
            scratch_shapes=[pltpu.VMEM((8, 8, 8, CH * L), f32)] * 7
            + [pltpu.SemaphoreType.DMA((20,)), pltpu.SemaphoreType.DMA((8,))],
            compiler_params=GRANT,
            name="combine",
        )(sums, b, z0, q0, w0, v0)

    field = P(GX, "gy", None, None)
    return jax.shard_map(
        body,
        mesh=fine,
        in_specs=(field, P(GX, "gy", None), P(GX, None)),
        out_specs=(field, field),
        check_vma=False,
    )
```

```python
import functools

import jax
import jax.numpy as jnp
from jax import lax
from jax.experimental import pallas as pl
from jax.experimental.pallas import tpu as pltpu
from jax.sharding import Mesh
from jax.sharding import PartitionSpec as P

OMEGA = 2.0 / 3.0
THIRD = 1.0 / 3.0
L = 128
CH = 4
HALO = 4
GX = ("z", "core")
SLAB2 = ("core", "gy")
ALL = ("z", "core", "gy")
HIGHEST = lax.Precision.HIGHEST
WHOLE = pltpu.CompilerParams(vmem_limit_bytes=(64 << 20) - (64 << 10))
GRANT = pltpu.CompilerParams(vmem_limit_bytes=(63 << 20) + (256 << 10))


def lanes():
    return lax.broadcasted_iota(jnp.int32, (8, L), 1)


def ld(ref, x, y):
    return [ref[x, y, :, k * L : (k + 1) * L] for k in range(CH)]


def row(ref, x, y):
    return [jnp.broadcast_to(ref[x, pl.ds(y, 1), k * L : (k + 1) * L], (8, L)) for k in range(CH)]


def put(ref, x, y, values):
    for k in range(CH):
        ref[x, y, :, k * L : (k + 1) * L] = values[k]


def zsum(v, lane):
    up = [pltpu.roll(c, 1, 1) for c in v]
    down = [pltpu.roll(c, L - 1, 1) for c in v]
    out = []
    for k in range(CH):
        before = up[k - 1] if k > 0 else jnp.zeros_like(up[0])
        after = down[k + 1] if k < CH - 1 else jnp.zeros_like(up[0])
        out.append(jnp.where(lane == 0, before, up[k]) + jnp.where(lane == L - 1, after, down[k]))
    return out


def add(*terms):
    return [functools.reduce(lambda a, b: a + b, t) for t in zip(*terms)]


def mul(a, b):
    return [p * q for p, q in zip(a, b)]


def scale(s, a):
    return [s * p for p in a]


def join(v):
    return jnp.concatenate(v, axis=1)


def beside_rows(ref, x, lo, hi, lane):
    prev, here = ld(ref, x, lo - 1), ld(ref, x, lo)
    for y in range(lo, hi):
        after = ld(ref, x, y + 1)
        near = add(prev, after, ld(ref, x - 1, y), ld(ref, x + 1, y), zsum(here, lane))
        yield y, here, near
        prev, here = here, after


def shares(h_ref, source, g_own, g_faces, rows_ref):
    lane = lanes()
    zero = [jnp.zeros((8, L), jnp.float32)] * CH

    def one_row(i, carry):
        a1, ylo, yhi = carry
        total = zero
        for y, here, near in beside_rows(h_ref, i + 1, 1, 9, lane):
            j = y - 1
            t1 = add(scale(THIRD, source(i, j)), near)
            s = mul(g_own(i, j), t1)
            a1 = add(a1, t1)
            total = add(total, s)
            if j == 0:
                ylo = add(ylo, s)
            if j == 7:
                yhi = add(yhi, s)
        for k in range(CH):
            rows_ref[i, :, k * L : (k + 1) * L] = total[k]
        return a1, ylo, yhi

    a1, ylo, yhi = lax.fori_loop(0, 8, one_row, (zero, zero, zero))
    rows = [[rows_ref[i, :, k * L : (k + 1) * L] for k in range(CH)] for i in range(8)]
    s_all = add(*rows)
    edges = (rows[0], rows[7], ylo, yhi)
    faces = []
    for f, (cells, edge) in enumerate(
        zip(
            (
                [(1, j + 1) for j in range(8)],
                [(8, j + 1) for j in range(8)],
                [(i + 1, 1) for i in range(8)],
                [(i + 1, 8) for i in range(8)],
            ),
            edges,
        )
    ):
        t_sum, s_sum = zero, zero
        for n, (x, y) in enumerate(cells):
            t = ld(h_ref, x, y)
            s = mul(g_faces(f, n), t)
            t_sum, s_sum = add(t_sum, t), add(s_sum, s)
            if n == 0:
                first = s
            if n == 7:
                last = s
        part = add(
            scale(THIRD, t_sum),
            edge,
            scale(3.0, s_sum),
            scale(-1.0, add(first, last)),
            zsum(s_sum, lane),
        )
        faces.append((part, s_sum, first, last))
    (xl, sxl, xl0, xl7), (xh, sxh, xh0, xh7), (yl, syl, yl0, yl7), (yh, syh, yh0, yh7) = faces
    own = add(
        scale(THIRD, a1),
        scale(4.0, s_all),
        scale(-1.0, add(*edges)),
        sxl,
        sxh,
        syl,
        syh,
        zsum(s_all, lane),
    )
    parts = [
        add(xl0, yl0),
        xl,
        add(xl7, yh0),
        yl,
        own,
        yh,
        add(xh0, yl7),
        xh,
        add(xh7, yh7),
    ]
    stacked = jnp.concatenate([join(p) for p in parts], axis=0)
    zi = lax.broadcasted_iota(jnp.int32, (CH * L, L), 0)
    li = lax.broadcasted_iota(jnp.int32, (CH * L, L), 1)
    fold = jnp.where((zi // 32) == (li % 16), 1.0 / 2048.0, 0.0)
    sums = jnp.dot(stacked, fold, precision=HIGHEST, preferred_element_type=jnp.float32)
    r = lax.broadcasted_iota(jnp.int32, (8, L), 0)
    keep = (lane // 16) == r
    out = [
        jnp.sum(jnp.where(keep, sums[8 * n : 8 * n + 8], 0.0), axis=0, keepdims=True)
        for n in range(9)
    ]
    return jnp.concatenate(out, axis=0)


def fill_border(ref):
    zero = jnp.zeros((8, CH * L), jnp.float32)

    def one(i, carry):
        ref[0, i] = zero
        ref[9, i] = zero
        ref[i, 0] = zero
        ref[i, 9] = zero
        return carry

    lax.fori_loop(0, 10, one, 0)


def first_shares_kernel(n_gx, n_gy, b_hbm, kap_hbm, kxl_hbm, kxh_hbm, ke_hbm, ko_hbm, out_ref, *refs):
    even, odd = parity()
    h_ref, g_ref, gf_ref, rows_ref, b_ref, KX, KY, sems = refs
    copies = run_copies(
        [
            (ke_hbm, KY.at[2 * even]),
            (kap_hbm, KY.at[1]),
            (ko_hbm, KY.at[2 * odd]),
            (kxl_hbm.at[7], KX.at[0]),
            (kxh_hbm.at[0], KX.at[1]),
        ]
        + [(b_hbm.at[2 * i : 2 * i + 2], b_ref.at[2 * i : 2 * i + 2]) for i in range(4)],
        sems,
    )
    has_x, has_y = place(n_gx, n_gy)
    fill_border(h_ref)
    for copy in copies[:5]:
        copy.wait()

    def one_row(i, carry):
        g_ref[i] = OMEGA / (6.0 + KY[1, i])
        gf_ref[2, pl.ds(i, 1)] = OMEGA / (6.0 + KY[0, i, 7:8]) * has_y[0]
        gf_ref[3, pl.ds(i, 1)] = OMEGA / (6.0 + KY[2, i, 0:1]) * has_y[2]
        for j in range(8):
            put(h_ref, i + 1, j + 1, mul(row(g_ref, i, j), ld(b_ref, i, j)))
        return carry

    for n in range(4):
        copies[5 + n].wait()
        lax.fori_loop(2 * n, 2 * n + 2, one_row, 0)
    gf_ref[0] = OMEGA / (6.0 + KX[0]) * has_x[0]
    gf_ref[1] = OMEGA / (6.0 + KX[1]) * has_x[2]
    out_ref[...] = shares(
        h_ref,
        lambda i, j: ld(b_ref, i, j),
        lambda i, j: row(g_ref, i, j),
        lambda f, n: row(gf_ref, f, n),
        rows_ref,
    )


def coarse_values(recv_ref, inv_ref, c_ref, count, valid):
    lane = lanes()
    r = lax.broadcasted_iota(jnp.int32, (8, L), 0)
    keep = (lane // 16) == r
    pieces = []
    for t in range(3):
        for j in range(count):
            value = None
            for dy in (-1, 0, 1):
                if not 0 <= j - dy < count:
                    continue
                for c in range(2):
                    term = recv_ref[c * count + j - dy, t * 3 + dy + 1]
                    value = term if value is None else value + term
            pieces.append(jnp.where(keep, jnp.broadcast_to(value, (8, L)), 0.0))
    i0 = lax.broadcasted_iota(jnp.int32, (L, L), 0)
    i1 = lax.broadcasted_iota(jnp.int32, (L, L), 1)
    fold = jnp.where((i0 % 16) == (i1 % 16), 1.0, 0.0)
    spread = jnp.dot(
        jnp.concatenate(pieces, axis=0), fold, precision=HIGHEST, preferred_element_type=jnp.float32
    )
    for t in range(3):
        values = []
        for part in range(0, count, 8):
            out = jnp.zeros((8, L), jnp.float32)
            for j in range(part, min(part + 8, count)):
                at = (t * count + j) * 8
                out = jnp.where((lane // 16) == j - part, spread[at : at + 8], out)
            values.append(out)
        d = jnp.concatenate(values, axis=1)[:, : count * 16]
        c = lax.dot_general(
            d,
            inv_ref[t],
            (((1,), (1,)), ((), ())),
            precision=HIGHEST,
            preferred_element_type=jnp.float32,
        )
        for jj in range(3):
            for k in range(CH):
                out = jnp.zeros((8, L), jnp.float32)
                for q in range(4):
                    m = jj * 16 + k * 4 + q
                    out = jnp.where((lane // 32) == q, jnp.broadcast_to(c[:, m : m + 1], (8, L)), out)
                c_ref[t * 3 + jj, :, k * L : (k + 1) * L] = out * (valid[0][t] * valid[1][jj])


def place(n_gx, n_gy):
    gx = lax.axis_index("z") * 2 + lax.axis_index("core")
    gy = lax.axis_index("gy")

    def flag(condition):
        return jnp.where(condition, 1.0, 0.0).astype(jnp.float32)

    one = jnp.float32(1.0)
    return (flag(gx > 0), one, flag(gx < n_gx - 1)), (flag(gy > 0), one, flag(gy < n_gy - 1))


def parity():
    odd = lax.rem(lax.axis_index("gy"), 2)
    return 1 - odd, odd


def run_copies(pairs, sems, base=0):
    copies = []
    for n, (src, dst) in enumerate(pairs):
        copy = pltpu.make_async_copy(src, dst, sems.at[base + n])
        copy.start()
        copies.append(copy)
    return copies


def pack_kernel(n_gy, cells, inverse, to_even, to_odd, m_high, m_low, b_ref, inv_ref, in_sems, sems):
    gy = lax.axis_index("gy")
    even, odd = parity()
    inv = []
    for n in range(6):
        block = jnp.clip(gy - 1 + n // 2, 0, n_gy - 1) * 16 + (n % 2) * 8
        half = (n % 2) * 256
        inv.append(
            (inverse.at[pl.ds(pl.multiple_of(block, 8), 8)], inv_ref.at[n // 2, :, half : half + 256])
        )
    for copy in run_copies([(cells, b_ref)] + inv, in_sems):
        copy.wait()
    pairs = []
    for x in range(8):
        pairs.append((b_ref.at[pl.ds(8 * x + 4 * even, 4)], to_even.at[x]))
        pairs.append((b_ref.at[pl.ds(8 * x + 4 * odd, 4)], to_odd.at[x]))
    for start, m in ((32, m_high), (0, m_low)):
        pairs.append((b_ref.at[start : start + 32], m.at[0:CELLS]))
        pairs.append((inv_ref, m.at[INV_AT:LAST]))
    for copy in run_copies(pairs, sems):
        copy.wait()


def pass_kernel(*refs):
    pass


CELLS, INV_AT, LAST = 32, 32, 35
HIGH_AT, KAPPA_AT, CORNERS = 6, 12, 18


def corner_segments():
    at = 0
    for a in (1, 2, 3):
        yield a, at, 4 - a
        at += 4 - a


def merge_kernel(first, n_z, n_gy, own_ref, low_ref, high_ref, y_even, y_odd, *refs):
    if first:
        k_even, k_odd = refs[:2]
        refs = refs[2:]
    out_ref, to_high, to_low, high_part, low_part, sems = refs
    even, odd = parity()
    sides = ((y_even, even, odd), (y_odd, odd, even))
    pairs = []
    for up, m in ((True, high_part), (False, low_part)):
        for a, at, wide in corner_segments():
            x = 8 - a if up else a - 1
            for face, above, below in sides:
                pairs.append(
                    (
                        face.at[pl.ds(x * 4 + below * (4 - wide), wide)],
                        m.at[pl.ds(at + above * HIGH_AT, wide)],
                    )
                )
        if first:
            x = 5 if up else 0
            pairs.append((k_even.at[x : x + 3], m.at[pl.ds(KAPPA_AT + 3 * even, 3)]))
            pairs.append((k_odd.at[x : x + 3], m.at[pl.ds(KAPPA_AT + 3 * odd, 3)]))
    copies = run_copies(pairs, sems)
    z, core = lax.axis_index("z"), lax.axis_index("core")
    below = jnp.where(z > 0, 1.0, 0.0).astype(jnp.float32)
    above = jnp.where(z < n_z - 1, 1.0, 0.0).astype(jnp.float32)
    own = [own_ref[n : n + 1] for n in range(9)]
    low = [low_ref[n : n + 1] * below for n in range(9)]
    high = [high_ref[n : n + 1] * above for n in range(9)]
    slabs = []
    for dy in range(3):
        first_core = [own[dy] + low[6 + dy], own[3 + dy], own[6 + dy] + high[dy], high[3 + dy]]
        second_core = [low[3 + dy], own[dy] + low[6 + dy], own[3 + dy], own[6 + dy] + high[dy]]
        slabs.append([jnp.where(core == 0, e, o) for e, o in zip(first_core, second_core)])
    for t in range(3):
        for dy in range(3):
            for n in range(n_gy):
                out_ref[n, 3 * t + dy] = slabs[dy][t]
                out_ref[n_gy + n, 3 * t + dy] = slabs[dy][t + 1]
    for copy in copies:
        copy.wait()
    for copy in run_copies([(high_part, to_high), (low_part, to_low)], sems):
        copy.wait()


def cycle_kernel(first, n_gx, n_gy, *refs):
    f_own, f_even, f_odd, f_xl, f_xh, f_cl, f_ch, b_xl, b_xh, b_cl, b_ch = refs[:11]
    kap_ref, kxl, kxh, k_even, k_odd, c_own, recv_ref = refs[11:18]
    refs = refs[18:]
    if first:
        z_out, q_out, dots_ref, out_ref = refs[:4]
        sends = refs[4:8]
        refs = refs[8:]
    else:
        extra_hbm, earlier_ref, z_out, q_out, dots_ref = refs[:5]
        refs = refs[5:]
    F, A, B, G, KC, KX, KY, inv_ref, c_ref, h_ref, gf_ref, rows_ref, z_ref, q_ref, extra_ref, sems = refs
    has_x, has_y = place(n_gx, n_gy)
    gy = lax.axis_index("gy")

    even, odd = parity()
    pairs = []
    for jj in range(3):
        block = jnp.clip(gy - 1 + jj, 0, n_gy - 1)
        pairs.append(
            (c_own.at[pl.ds(pl.multiple_of(block * 16, 16), 16)], inv_ref.at[1, jj * 16 : jj * 16 + 16])
        )
    for t, ref in ((0, b_xl), (2, b_xh)):
        for n in range(6):
            half = (n % 2) * 256
            pairs.append((ref.at[INV_AT + n // 2, :, half : half + 256], inv_ref.at[t, n * 8 : n * 8 + 8]))
    n_inv = len(pairs)
    pairs += [
        (b_cl.at[KAPPA_AT:CORNERS], KC.at[0]),
        (b_ch.at[KAPPA_AT:CORNERS], KC.at[1]),
        (kap_ref, KY.at[1]),
        (k_even, KY.at[2 * even]),
        (k_odd, KY.at[2 * odd]),
        (kxl.at[4:8], KX.at[0]),
        (kxh.at[0:4], KX.at[1]),
    ]
    n_kappa = len(pairs)
    pairs += [
        (f_own, F.at[4:12, 4:12]),
        (f_even, F.at[4:12, pl.ds(12 * even, 4)]),
        (f_odd, F.at[4:12, pl.ds(12 * odd, 4)]),
    ]
    for low, ref, corner in ((True, f_xl, f_cl), (False, f_xh, f_ch)):
        for i in range(4):
            pairs.append((ref.at[8 * i : 8 * i + 8], F.at[i if low else 12 + i, 4:12]))
        for a, at, wide in corner_segments():
            x = 4 - a if low else 11 + a
            pairs.append((corner.at[at : at + wide], F.at[x, 4 - wide : 4]))
            pairs.append((corner.at[HIGH_AT + at : HIGH_AT + at + wide], F.at[x, 12 : 12 + wide]))
    n_field = len(pairs)
    if not first:
        pairs.append((extra_hbm, extra_ref))
    copies = run_copies(pairs, sems)

    zero = jnp.zeros((8, CH * L), jnp.float32)
    for x, y in [(a, b) for a in range(4) for b in range(4) if (4 - a) + (4 - b) > 4]:
        for xx, yy in ((x, y), (x, 15 - y), (15 - x, y), (15 - x, 15 - y)):
            F[xx, yy] = zero

    def inv_diag(kappa):
        return OMEGA / (6.0 + kappa)

    for copy in copies[:n_inv]:
        copy.wait()
    coarse_values(recv_ref, inv_ref, c_ref, n_gy, (has_x, has_y))

    for copy in copies[n_inv:n_kappa]:
        copy.wait()
    for i in range(8):
        G[4 + i, 8:16] = inv_diag(KY[1, i])
        G[4 + i, 0:8] = inv_diag(KY[0, i]) * has_y[0]
        G[4 + i, 16:24] = inv_diag(KY[2, i]) * has_y[2]
    for a in range(4):
        G[a, 8:16] = inv_diag(KX[0, a]) * has_x[0]
        G[12 + a, 8:16] = inv_diag(KX[1, a]) * has_x[2]
    for side, sx in ((0, -1), (1, 1)):
        for half, sy in ((0, -1), (1, 1)):
            mask = has_x[1 + sx] * has_y[1 + sy]
            y = 0 if sy < 0 else 16
            G[0 if sx < 0 else 15, y : y + 8] = zero
            for i in range(3):
                G[1 + i if sx < 0 else 12 + i, y : y + 8] = inv_diag(KC[side, 3 * half + i]) * mask
    for copy in copies[n_kappa:n_field]:
        copy.wait()

    lane = lanes()

    def start_row(x, carry):
        for y in range(16):
            put(A, x, y, mul(row(G, x, y + 4), ld(F, x, y)))
        return carry

    lax.fori_loop(0, 16, start_row, 0)

    def sweep(src, dst, width, coarse):
        def one_row(x, reach):
            t = jnp.where(x >= 4, 1, 0) + jnp.where(x >= 12, 1, 0)
            for y, here, near in beside_rows(src, x, 4 - reach, 12 + reach, lane):
                new = add(scale(THIRD, here), mul(add(ld(F, x, y), near), row(G, x, y + 4)))
                if coarse:
                    jj = (1 if y >= 4 else 0) + (1 if y >= 12 else 0)
                    new = add(new, [c_ref[t * 3 + jj, :, k * L : (k + 1) * L] for k in range(CH)])
                put(dst, x, y, new)

        def inner(x, carry):
            one_row(x, width)
            return carry

        for a in range(1, width + 1):
            one_row(4 - a, width - a)
            one_row(11 + a, width - a)
        lax.fori_loop(4, 12, inner, 0, unroll=2)

    sweep(A, B, 3, True)
    sweep(B, A, 2, False)
    sweep(A, B, 1, False)
    for copy in copies[n_field:]:
        copy.wait()
    if first:
        fill_border(h_ref)
    nil = jnp.zeros((8, L), jnp.float32)

    def image_row(i, carry):
        fz, zq, ez = carry
        x = i + 4
        for y, here, near in beside_rows(B, x, 4, 12, lane):
            j = y - 4
            kappa = row(KY.at[1], i, j)
            image = [(6.0 + kappa[k]) * here[k] - near[k] for k in range(CH)]
            put(z_ref, i, j, here)
            put(q_ref, i, j, image)
            source = ld(F, x, y)
            fz = functools.reduce(lambda a, b: a + b, mul(source, here), fz)
            zq = functools.reduce(lambda a, b: a + b, mul(here, image), zq)
            if first:
                put(h_ref, i + 1, j + 1, mul(row(G, x, y + 4), image))
            else:
                ez = functools.reduce(lambda a, b: a + b, mul(ld(extra_ref, i, j), here), ez)
        return fz, zq, ez

    fz, zq, ez = lax.fori_loop(0, 8, image_row, (nil, nil, nil))
    if first:
        dots_ref[0] = fz
        dots_ref[1] = zq
        copies = run_copies(
            [
                (q_ref.at[0:8, pl.ds(4 * even, 4)], sends[0]),
                (q_ref.at[0:8, pl.ds(4 * odd, 4)], sends[1]),
            ]
            + [(q_ref.at[4 + i], sends[2].at[8 * i : 8 * i + 8]) for i in range(4)]
            + [(q_ref.at[i], sends[3].at[8 * i : 8 * i + 8]) for i in range(4)]
            + [
                (q_ref, q_out),
                (z_ref, z_out),
            ],
            sems,
        )
        gf_ref[0] = G[3, 8:16]
        gf_ref[1] = G[12, 8:16]
        for i in range(8):
            gf_ref[2, pl.ds(i, 1)] = G[4 + i, 7:8]
            gf_ref[3, pl.ds(i, 1)] = G[4 + i, 16:17]
        out_ref[...] = shares(
            h_ref,
            lambda i, j: ld(q_ref, i, j),
            lambda i, j: row(G, i + 4, j + 8),
            lambda f, n: row(gf_ref, f, n),
            rows_ref,
        )
        for copy in copies:
            copy.wait()
    else:
        copies = run_copies([(z_ref, z_out), (q_ref, q_out)], sems)
        total = [earlier_ref[0], earlier_ref[1], fz, zq, ez]
        packed = nil
        sub = lax.broadcasted_iota(jnp.int32, (8, L), 0)
        for k, part in enumerate(total):
            packed = jnp.where(lane == 8 * k + sub, jnp.sum(part, axis=1, keepdims=True), packed)
        packed = jnp.sum(packed, axis=0, keepdims=True)
        for n in range(2 * n_gy):
            dots_ref[n] = packed
        for copy in copies:
            copy.wait()


def combine_kernel(sums_ref, *refs):
    sources, outs = refs[:5], refs[5:7]
    b_ref, z_ref, q_ref, w_ref, v_ref = refs[7:12]
    x_keep, r_keep, in_sems, sems = refs[12:]
    fetched = [
        run_copies(
            [(src.at[2 * i : 2 * i + 2], dst.at[2 * i : 2 * i + 2]) for src, dst in zip(sources, refs[7:12])],
            in_sems,
            5 * i,
        )
        for i in range(4)
    ]
    sums = sums_ref[0]
    for n in range(1, sums_ref.shape[0]):
        sums = sums + sums_ref[n]
    sums = jnp.broadcast_to(sums, (8, L))
    sub = lax.broadcasted_iota(jnp.int32, (8, L), 0)
    bz, zq, qw, wv, bw = (
        jnp.sum(jnp.where(lanes() == 8 * k + sub, sums, 0.0), axis=1, keepdims=True) for k in range(5)
    )
    a0 = bz / zq
    e1 = bz - a0 * (bw + zq) + a0 * a0 * qw
    beta = e1 / bz
    z1q = zq - a0 * qw
    z1v = zq - 2.0 * a0 * qw + a0 * a0 * wv
    a1 = e1 / (z1v + 2.0 * beta * z1q + beta * beta * zq)
    cz = jnp.broadcast_to(a0 + a1 * (1.0 + beta), (8, CH * L))
    cw = jnp.broadcast_to(a1 * a0, (8, CH * L))
    copies = []
    for n in range(4):
        for copy in fetched[n]:
            copy.wait()
        for i in (2 * n, 2 * n + 1):
            for j in range(8):
                x_keep[i, j] = cz * z_ref[i, j] - cw * w_ref[i, j]
                r_keep[i, j] = b_ref[i, j] - cz * q_ref[i, j] + cw * v_ref[i, j]
        part = slice(2 * n, 2 * n + 2)
        copies += run_copies([(x_keep.at[part], outs[0].at[part]), (r_keep.at[part], outs[1].at[part])], sems, 2 * n)
    for copy in copies:
        copy.wait()


def shift(value, axes, sizes, steps):
    pairs = []
    total = 1
    for n in sizes:
        total *= n
    for flat in range(total):
        rest, target = flat, 0
        weight = 1
        for n, step in zip(reversed(sizes), reversed(steps)):
            at = rest % n
            rest //= n
            target += ((at + step) % n) * weight
            weight *= n
        pairs.append((flat, target))
    return lax.ppermute(value, axes, pairs)


VM = pl.BlockSpec(memory_space=pltpu.VMEM)
HB = pl.BlockSpec(memory_space=pl.ANY)


def solution(mesh):
    n_gx, n_gy = mesh.shape["gx"], mesh.shape["gy"]
    n_z = n_gx // 2
    fine = Mesh(mesh.devices.reshape(n_z, 2, n_gy), ALL)

    f32 = jnp.float32

    def shape(*dims):
        return jax.ShapeDtypeStruct(dims, f32)

    tile = shape(8, 8, 8, CH * L)
    y_face = shape(8, 4, 8, CH * L)

    even_pairs = [(n, n ^ 1) for n in range(n_gy)]
    odd_pairs = [(n, ((n - 1) ^ 1) + 1 if 0 < n < n_gy - 1 else n) for n in range(n_gy)]

    def along_gy(to_even, to_odd):
        return [lax.ppermute(to_even, "gy", even_pairs), lax.ppermute(to_odd, "gy", odd_pairs)]

    def after(first, then):
        return pl.pallas_call(
            pass_kernel,
            out_shape=[shape(*v.shape) for v in then],
            in_specs=[HB] * (len(first) + len(then)),
            out_specs=[HB] * len(then),
            input_output_aliases={len(first) + n: n for n in range(len(then))},
            compiler_params=WHOLE,
            name="pass_on",
        )(*first, *then)

    def along_gx(to_high, to_low):
        return [shift(to_high, GX, (n_gx,), (1,)), shift(to_low, GX, (n_gx,), (-1,))]

    def exchange(own, faces, messages, more):
        low = shift(own, ("z",), (n_z,), (1,))
        high = shift(own, ("z",), (n_z,), (-1,))
        cells = along_gx(*after((low, high), messages))
        size = CORNERS if more else KAPPA_AT
        part = pltpu.VMEM((size, 8, CH * L), f32)
        out, to_high, to_low = pl.pallas_call(
            functools.partial(merge_kernel, bool(more), n_z, n_gy),
            out_shape=[shape(2 * n_gy, 9, 1, L)] + [shape(size, 8, CH * L)] * 2,
            in_specs=[VM] * 3 + [HB] * (2 + len(more)),
            out_specs=[VM, HB, HB],
            scratch_shapes=[part, part, pltpu.SemaphoreType.DMA((20,))],
            compiler_params=GRANT,
            name="merge_shares",
        )(own, low, high, *(f.reshape(32, 8, CH * L) for f in faces), *more)
        corners = along_gx(to_high, to_low)
        return lax.all_to_all(out, SLAB2, 0, 0), cells + corners

    def body(b, kappa, inverse):
        around = [
            shift(kappa, GX, (n_gx,), (1,)),
            shift(kappa, GX, (n_gx,), (-1,)),
            *along_gy(kappa, kappa),
        ]
        packed = pl.pallas_call(
            functools.partial(pack_kernel, n_gy),
            out_shape=[y_face, y_face] + [shape(LAST, 8, CH * L)] * 2,
            in_specs=[HB, HB],
            out_specs=[HB] * 4,
            scratch_shapes=[
                pltpu.VMEM((64, 8, CH * L), f32),
                pltpu.VMEM((3, 8, CH * L), f32),
                pltpu.SemaphoreType.DMA((7,)),
                pltpu.SemaphoreType.DMA((20,)),
            ],
            compiler_params=WHOLE,
            name="pack_faces",
        )(b.reshape(64, 8, CH * L), inverse)
        behind = after(around, packed[:2])
        b_faces = along_gy(*behind)
        own = pl.pallas_call(
            functools.partial(first_shares_kernel, n_gx, n_gy),
            out_shape=shape(9, L),
            in_specs=[HB] * 6,
            out_specs=VM,
            scratch_shapes=[
                pltpu.VMEM((10, 10, 8, CH * L), f32),
                pltpu.VMEM((8, 8, CH * L), f32),
                pltpu.VMEM((4, 8, CH * L), f32),
                pltpu.VMEM((8, 8, CH * L), f32),
                pltpu.VMEM((8, 8, 8, CH * L), f32),
                pltpu.VMEM((2, 8, CH * L), f32),
                pltpu.VMEM((3, 8, 8, CH * L), f32),
                pltpu.SemaphoreType.DMA((9,)),
            ],
            compiler_params=GRANT,
            name="first_shares",
        )(b, kappa, *around)

        def cycle(first, field, faces, messages, b_messages, received, more):
            outs = [tile, tile]
            out_specs = [HB, HB, VM]
            if first:
                outs += [shape(2, 8, L), shape(9, L), y_face, y_face]
                outs += [shape(CELLS, 8, CH * L)] * 2
                out_specs += [VM, HB, HB, HB, HB]
            else:
                outs += [shape(2 * n_gy, 1, L)]
            big = pltpu.VMEM((16, 16, 8, CH * L), f32)
            own_tile = pltpu.VMEM((8, 8, 8, CH * L), f32)
            return pl.pallas_call(
                functools.partial(cycle_kernel, first, n_gx, n_gy),
                out_shape=outs,
                in_specs=[HB] * 17 + [VM] + ([HB, VM] if more else []),
                out_specs=out_specs,
                scratch_shapes=[
                    big,
                    big,
                    big,
                    pltpu.VMEM((16, 24, CH * L), f32),
                    pltpu.VMEM((2, 6, 8, CH * L), f32),
                    pltpu.VMEM((2, 4, 8, CH * L), f32),
                    pltpu.VMEM((3, 8, 8, CH * L), f32),
                    pltpu.VMEM((3, 48, 16 * n_gy), f32),
                    pltpu.VMEM((9, 8, CH * L), f32),
                    pltpu.VMEM((10, 10, 8, CH * L), f32),
                    pltpu.VMEM((4, 8, CH * L), f32),
                    pltpu.VMEM((8, 8, CH * L), f32),
                    own_tile,
                    own_tile,
                    own_tile,
                    pltpu.SemaphoreType.DMA((52,)),
                ],
                compiler_params=GRANT,
                name="first_cycle" if first else "second_cycle",
            )(field, *faces, *messages, *b_messages, kappa, *around, inverse, received, *more)

        received, b_messages = exchange(own, b_faces, packed[2:], around[2:])
        z0, q0, dots, own, *sends = cycle(True, b, b_faces, b_messages, b_messages, received, [])
        q_faces = along_gy(*sends[:2])
        received, messages = exchange(own, q_faces, sends[2:], [])
        w0, v0, packed = cycle(False, q0, q_faces, messages, b_messages, received, [b, dots])

        near_sum = jnp.sum(lax.all_to_all(packed, SLAB2, 0, 0), axis=0)
        sums = lax.all_to_all(jnp.broadcast_to(near_sum, (n_z, 1, L)), "z", 0, 0)
        return pl.pallas_call(
            combine_kernel,
            out_shape=[tile, tile],
            in_specs=[VM] + [HB] * 5,
            out_specs=[HB, HB],
            scratch_shapes=[pltpu.VMEM((8, 8, 8, CH * L), f32)] * 7
            + [pltpu.SemaphoreType.DMA((20,)), pltpu.SemaphoreType.DMA((8,))],
            compiler_params=GRANT,
            name="combine",
        )(sums, b, z0, q0, w0, v0)

    field = P(GX, "gy", None, None)
    return jax.shard_map(
        body,
        mesh=fine,
        in_specs=(field, P(GX, "gy", None), P(GX, None)),
        out_specs=(field, field),
        check_vma=False,
    )
```

```python
import functools

import jax
import jax.numpy as jnp
from jax import lax
from jax.experimental import pallas as pl
from jax.experimental.pallas import tpu as pltpu
from jax.sharding import Mesh
from jax.sharding import PartitionSpec as P

OMEGA = 2.0 / 3.0
THIRD = 1.0 / 3.0
L = 128
CH = 4
HALO = 4
GX = ("z", "core")
SLAB2 = ("core", "gy")
ALL = ("z", "core", "gy")
HIGHEST = lax.Precision.HIGHEST
WHOLE = pltpu.CompilerParams(vmem_limit_bytes=(64 << 20) - (64 << 10))
GRANT = pltpu.CompilerParams(vmem_limit_bytes=(63 << 20) + (256 << 10))


def lanes():
    return lax.broadcasted_iota(jnp.int32, (8, L), 1)


def ld(ref, x, y):
    return [ref[x, y, :, k * L : (k + 1) * L] for k in range(CH)]


def row(ref, x, y):
    return [jnp.broadcast_to(ref[x, pl.ds(y, 1), k * L : (k + 1) * L], (8, L)) for k in range(CH)]


def put(ref, x, y, values):
    for k in range(CH):
        ref[x, y, :, k * L : (k + 1) * L] = values[k]


def zsum(v, lane):
    up = [pltpu.roll(c, 1, 1) for c in v]
    down = [pltpu.roll(c, L - 1, 1) for c in v]
    out = []
    for k in range(CH):
        before = up[k - 1] if k > 0 else jnp.zeros_like(up[0])
        after = down[k + 1] if k < CH - 1 else jnp.zeros_like(up[0])
        out.append(jnp.where(lane == 0, before, up[k]) + jnp.where(lane == L - 1, after, down[k]))
    return out


def add(*terms):
    return [functools.reduce(lambda a, b: a + b, t) for t in zip(*terms)]


def mul(a, b):
    return [p * q for p, q in zip(a, b)]


def scale(s, a):
    return [s * p for p in a]


def join(v):
    return jnp.concatenate(v, axis=1)


def beside_rows(ref, x, lo, hi, lane):
    prev, here = ld(ref, x, lo - 1), ld(ref, x, lo)
    for y in range(lo, hi):
        after = ld(ref, x, y + 1)
        near = add(prev, after, ld(ref, x - 1, y), ld(ref, x + 1, y), zsum(here, lane))
        yield y, here, near
        prev, here = here, after


def shares(h_ref, source, g_own, g_faces, rows_ref):
    lane = lanes()
    zero = [jnp.zeros((8, L), jnp.float32)] * CH

    def one_row(i, carry):
        a1, ylo, yhi = carry
        total = zero
        for y, here, near in beside_rows(h_ref, i + 1, 1, 9, lane):
            j = y - 1
            t1 = add(scale(THIRD, source(i, j)), near)
            s = mul(g_own(i, j), t1)
            a1 = add(a1, t1)
            total = add(total, s)
            if j == 0:
                ylo = add(ylo, s)
            if j == 7:
                yhi = add(yhi, s)
        for k in range(CH):
            rows_ref[i, :, k * L : (k + 1) * L] = total[k]
        return a1, ylo, yhi

    a1, ylo, yhi = lax.fori_loop(0, 8, one_row, (zero, zero, zero), unroll=2)
    rows = [[rows_ref[i, :, k * L : (k + 1) * L] for k in range(CH)] for i in range(8)]
    s_all = add(*rows)
    edges = (rows[0], rows[7], ylo, yhi)
    faces = []
    for f, (cells, edge) in enumerate(
        zip(
            (
                [(1, j + 1) for j in range(8)],
                [(8, j + 1) for j in range(8)],
                [(i + 1, 1) for i in range(8)],
                [(i + 1, 8) for i in range(8)],
            ),
            edges,
        )
    ):
        t_sum, s_sum = zero, zero
        for n, (x, y) in enumerate(cells):
            t = ld(h_ref, x, y)
            s = mul(g_faces(f, n), t)
            t_sum, s_sum = add(t_sum, t), add(s_sum, s)
            if n == 0:
                first = s
            if n == 7:
                last = s
        part = add(
            scale(THIRD, t_sum),
            edge,
            scale(3.0, s_sum),
            scale(-1.0, add(first, last)),
            zsum(s_sum, lane),
        )
        faces.append((part, s_sum, first, last))
    (xl, sxl, xl0, xl7), (xh, sxh, xh0, xh7), (yl, syl, yl0, yl7), (yh, syh, yh0, yh7) = faces
    own = add(
        scale(THIRD, a1),
        scale(4.0, s_all),
        scale(-1.0, add(*edges)),
        sxl,
        sxh,
        syl,
        syh,
        zsum(s_all, lane),
    )
    parts = [
        add(xl0, yl0),
        xl,
        add(xl7, yh0),
        yl,
        own,
        yh,
        add(xh0, yl7),
        xh,
        add(xh7, yh7),
    ]
    stacked = jnp.concatenate([join(p) for p in parts], axis=0)
    zi = lax.broadcasted_iota(jnp.int32, (CH * L, L), 0)
    li = lax.broadcasted_iota(jnp.int32, (CH * L, L), 1)
    fold = jnp.where((zi // 32) == (li % 16), 1.0 / 2048.0, 0.0)
    sums = jnp.dot(stacked, fold, precision=HIGHEST, preferred_element_type=jnp.float32)
    r = lax.broadcasted_iota(jnp.int32, (8, L), 0)
    keep = (lane // 16) == r
    out = [
        jnp.sum(jnp.where(keep, sums[8 * n : 8 * n + 8], 0.0), axis=0, keepdims=True)
        for n in range(9)
    ]
    return jnp.concatenate(out, axis=0)


def fill_border(ref):
    zero = jnp.zeros((8, CH * L), jnp.float32)

    def one(i, carry):
        ref[0, i] = zero
        ref[9, i] = zero
        ref[i, 0] = zero
        ref[i, 9] = zero
        return carry

    lax.fori_loop(0, 10, one, 0)


def first_shares_kernel(n_gx, n_gy, b_hbm, kap_hbm, kxl_hbm, kxh_hbm, ke_hbm, ko_hbm, out_ref, *refs):
    even, odd = parity()
    h_ref, g_ref, gf_ref, rows_ref, b_ref, KX, KY, sems = refs
    copies = run_copies(
        [
            (ke_hbm, KY.at[2 * even]),
            (kap_hbm, KY.at[1]),
            (ko_hbm, KY.at[2 * odd]),
            (kxl_hbm.at[7], KX.at[0]),
            (kxh_hbm.at[0], KX.at[1]),
        ]
        + [(b_hbm.at[2 * i : 2 * i + 2], b_ref.at[2 * i : 2 * i + 2]) for i in range(4)],
        sems,
    )
    has_x, has_y = place(n_gx, n_gy)
    fill_border(h_ref)
    for copy in copies[:5]:
        copy.wait()

    def one_row(i, carry):
        g_ref[i] = OMEGA / (6.0 + KY[1, i])
        gf_ref[2, pl.ds(i, 1)] = OMEGA / (6.0 + KY[0, i, 7:8]) * has_y[0]
        gf_ref[3, pl.ds(i, 1)] = OMEGA / (6.0 + KY[2, i, 0:1]) * has_y[2]
        for j in range(8):
            put(h_ref, i + 1, j + 1, mul(row(g_ref, i, j), ld(b_ref, i, j)))
        return carry

    for n in range(4):
        copies[5 + n].wait()
        lax.fori_loop(2 * n, 2 * n + 2, one_row, 0)
    gf_ref[0] = OMEGA / (6.0 + KX[0]) * has_x[0]
    gf_ref[1] = OMEGA / (6.0 + KX[1]) * has_x[2]
    out_ref[...] = shares(
        h_ref,
        lambda i, j: ld(b_ref, i, j),
        lambda i, j: row(g_ref, i, j),
        lambda f, n: row(gf_ref, f, n),
        rows_ref,
    )


def coarse_values(recv_ref, inv_ref, c_ref, count, valid):
    lane = lanes()
    r = lax.broadcasted_iota(jnp.int32, (8, L), 0)
    keep = (lane // 16) == r
    pieces = []
    for t in range(3):
        for j in range(count):
            value = None
            for dy in (-1, 0, 1):
                if not 0 <= j - dy < count:
                    continue
                for c in range(2):
                    term = recv_ref[c * count + j - dy, t * 3 + dy + 1]
                    value = term if value is None else value + term
            pieces.append(jnp.where(keep, jnp.broadcast_to(value, (8, L)), 0.0))
    i0 = lax.broadcasted_iota(jnp.int32, (L, L), 0)
    i1 = lax.broadcasted_iota(jnp.int32, (L, L), 1)
    fold = jnp.where((i0 % 16) == (i1 % 16), 1.0, 0.0)
    spread = jnp.dot(
        jnp.concatenate(pieces, axis=0), fold, precision=HIGHEST, preferred_element_type=jnp.float32
    )
    for t in range(3):
        values = []
        for part in range(0, count, 8):
            out = jnp.zeros((8, L), jnp.float32)
            for j in range(part, min(part + 8, count)):
                at = (t * count + j) * 8
                out = jnp.where((lane // 16) == j - part, spread[at : at + 8], out)
            values.append(out)
        d = jnp.concatenate(values, axis=1)[:, : count * 16]
        c = lax.dot_general(
            d,
            inv_ref[t],
            (((1,), (1,)), ((), ())),
            precision=HIGHEST,
            preferred_element_type=jnp.float32,
        )
        for jj in range(3):
            for k in range(CH):
                out = jnp.zeros((8, L), jnp.float32)
                for q in range(4):
                    m = jj * 16 + k * 4 + q
                    out = jnp.where((lane // 32) == q, jnp.broadcast_to(c[:, m : m + 1], (8, L)), out)
                c_ref[t * 3 + jj, :, k * L : (k + 1) * L] = out * (valid[0][t] * valid[1][jj])


def place(n_gx, n_gy):
    gx = lax.axis_index("z") * 2 + lax.axis_index("core")
    gy = lax.axis_index("gy")

    def flag(condition):
        return jnp.where(condition, 1.0, 0.0).astype(jnp.float32)

    one = jnp.float32(1.0)
    return (flag(gx > 0), one, flag(gx < n_gx - 1)), (flag(gy > 0), one, flag(gy < n_gy - 1))


def parity():
    odd = lax.rem(lax.axis_index("gy"), 2)
    return 1 - odd, odd


def run_copies(pairs, sems, base=0):
    copies = []
    for n, (src, dst) in enumerate(pairs):
        copy = pltpu.make_async_copy(src, dst, sems.at[base + n])
        copy.start()
        copies.append(copy)
    return copies


def pack_kernel(n_gy, cells, inverse, to_even, to_odd, m_high, m_low, b_ref, inv_ref, in_sems, sems):
    gy = lax.axis_index("gy")
    even, odd = parity()
    inv = []
    for n in range(6):
        block = jnp.clip(gy - 1 + n // 2, 0, n_gy - 1) * 16 + (n % 2) * 8
        half = (n % 2) * 256
        inv.append(
            (inverse.at[pl.ds(pl.multiple_of(block, 8), 8)], inv_ref.at[n // 2, :, half : half + 256])
        )
    for copy in run_copies([(cells, b_ref)] + inv, in_sems):
        copy.wait()
    pairs = []
    for x in range(8):
        pairs.append((b_ref.at[pl.ds(8 * x + 4 * even, 4)], to_even.at[x]))
        pairs.append((b_ref.at[pl.ds(8 * x + 4 * odd, 4)], to_odd.at[x]))
    for start, m in ((32, m_high), (0, m_low)):
        pairs.append((b_ref.at[start : start + 32], m.at[0:CELLS]))
        pairs.append((inv_ref, m.at[INV_AT:LAST]))
    for copy in run_copies(pairs, sems):
        copy.wait()


def pass_kernel(*refs):
    pass


CELLS, INV_AT, LAST = 32, 32, 35
HIGH_AT, KAPPA_AT, CORNERS = 6, 12, 18


def corner_segments():
    at = 0
    for a in (1, 2, 3):
        yield a, at, 4 - a
        at += 4 - a


def merge_kernel(first, n_z, n_gy, own_ref, low_ref, high_ref, y_even, y_odd, *refs):
    if first:
        k_even, k_odd = refs[:2]
        refs = refs[2:]
    out_ref, to_high, to_low, high_part, low_part, sems = refs
    even, odd = parity()
    sides = ((y_even, even, odd), (y_odd, odd, even))
    pairs = []
    for up, m in ((True, high_part), (False, low_part)):
        for a, at, wide in corner_segments():
            x = 8 - a if up else a - 1
            for face, above, below in sides:
                pairs.append(
                    (
                        face.at[pl.ds(x * 4 + below * (4 - wide), wide)],
                        m.at[pl.ds(at + above * HIGH_AT, wide)],
                    )
                )
        if first:
            x = 5 if up else 0
            pairs.append((k_even.at[x : x + 3], m.at[pl.ds(KAPPA_AT + 3 * even, 3)]))
            pairs.append((k_odd.at[x : x + 3], m.at[pl.ds(KAPPA_AT + 3 * odd, 3)]))
    copies = run_copies(pairs, sems)
    z, core = lax.axis_index("z"), lax.axis_index("core")
    below = jnp.where(z > 0, 1.0, 0.0).astype(jnp.float32)
    above = jnp.where(z < n_z - 1, 1.0, 0.0).astype(jnp.float32)
    own = [own_ref[n : n + 1] for n in range(9)]
    low = [low_ref[n : n + 1] * below for n in range(9)]
    high = [high_ref[n : n + 1] * above for n in range(9)]
    slabs = []
    for dy in range(3):
        first_core = [own[dy] + low[6 + dy], own[3 + dy], own[6 + dy] + high[dy], high[3 + dy]]
        second_core = [low[3 + dy], own[dy] + low[6 + dy], own[3 + dy], own[6 + dy] + high[dy]]
        slabs.append([jnp.where(core == 0, e, o) for e, o in zip(first_core, second_core)])
    for t in range(3):
        for dy in range(3):
            for n in range(n_gy):
                out_ref[n, 3 * t + dy] = slabs[dy][t]
                out_ref[n_gy + n, 3 * t + dy] = slabs[dy][t + 1]
    for copy in copies:
        copy.wait()
    for copy in run_copies([(high_part, to_high), (low_part, to_low)], sems):
        copy.wait()


def cycle_kernel(first, n_gx, n_gy, *refs):
    f_own, f_even, f_odd, f_xl, f_xh, f_cl, f_ch, b_xl, b_xh, b_cl, b_ch = refs[:11]
    kap_ref, kxl, kxh, k_even, k_odd, c_own, recv_hbm = refs[11:18]
    refs = refs[18:]
    if first:
        z_out, q_out, dots_ref, out_ref = refs[:4]
        sends = refs[4:8]
        refs = refs[8:]
    else:
        extra_hbm, earlier_ref, z_out, q_out, dots_ref = refs[:5]
        refs = refs[5:]
    F, A, B, G, KC, KX, KY, inv_ref, c_ref, h_ref, gf_ref, rows_ref, z_ref, q_ref, extra_ref, recv_ref, sems = refs
    has_x, has_y = place(n_gx, n_gy)
    gy = lax.axis_index("gy")

    even, odd = parity()
    pairs = [(recv_hbm, recv_ref)]
    for jj in range(3):
        block = jnp.clip(gy - 1 + jj, 0, n_gy - 1)
        pairs.append(
            (c_own.at[pl.ds(pl.multiple_of(block * 16, 16), 16)], inv_ref.at[1, jj * 16 : jj * 16 + 16])
        )
    for t, ref in ((0, b_xl), (2, b_xh)):
        for n in range(6):
            half = (n % 2) * 256
            pairs.append((ref.at[INV_AT + n // 2, :, half : half + 256], inv_ref.at[t, n * 8 : n * 8 + 8]))
    n_inv = len(pairs)
    pairs += [
        (b_cl.at[KAPPA_AT:CORNERS], KC.at[0]),
        (b_ch.at[KAPPA_AT:CORNERS], KC.at[1]),
        (kap_ref, KY.at[1]),
        (k_even, KY.at[2 * even]),
        (k_odd, KY.at[2 * odd]),
        (kxl.at[4:8], KX.at[0]),
        (kxh.at[0:4], KX.at[1]),
    ]
    n_kappa = len(pairs)
    pairs += [
        (f_own, F.at[4:12, 4:12]),
        (f_even, F.at[4:12, pl.ds(12 * even, 4)]),
        (f_odd, F.at[4:12, pl.ds(12 * odd, 4)]),
    ]
    for low, ref, corner in ((True, f_xl, f_cl), (False, f_xh, f_ch)):
        for i in range(4):
            pairs.append((ref.at[8 * i : 8 * i + 8], F.at[i if low else 12 + i, 4:12]))
        for a, at, wide in corner_segments():
            x = 4 - a if low else 11 + a
            pairs.append((corner.at[at : at + wide], F.at[x, 4 - wide : 4]))
            pairs.append((corner.at[HIGH_AT + at : HIGH_AT + at + wide], F.at[x, 12 : 12 + wide]))
    n_field = len(pairs)
    if not first:
        pairs.append((extra_hbm, extra_ref))
    copies = run_copies(pairs, sems)

    zero = jnp.zeros((8, CH * L), jnp.float32)
    for x, y in [(a, b) for a in range(4) for b in range(4) if (4 - a) + (4 - b) > 4]:
        for xx, yy in ((x, y), (x, 15 - y), (15 - x, y), (15 - x, 15 - y)):
            F[xx, yy] = zero

    def inv_diag(kappa):
        return OMEGA / (6.0 + kappa)

    for copy in copies[:n_inv]:
        copy.wait()
    coarse_values(recv_ref, inv_ref, c_ref, n_gy, (has_x, has_y))

    for copy in copies[n_inv:n_kappa]:
        copy.wait()
    for i in range(8):
        G[4 + i, 8:16] = inv_diag(KY[1, i])
        G[4 + i, 0:8] = inv_diag(KY[0, i]) * has_y[0]
        G[4 + i, 16:24] = inv_diag(KY[2, i]) * has_y[2]
    for a in range(4):
        G[a, 8:16] = inv_diag(KX[0, a]) * has_x[0]
        G[12 + a, 8:16] = inv_diag(KX[1, a]) * has_x[2]
    for side, sx in ((0, -1), (1, 1)):
        for half, sy in ((0, -1), (1, 1)):
            mask = has_x[1 + sx] * has_y[1 + sy]
            y = 0 if sy < 0 else 16
            G[0 if sx < 0 else 15, y : y + 8] = zero
            for i in range(3):
                G[1 + i if sx < 0 else 12 + i, y : y + 8] = inv_diag(KC[side, 3 * half + i]) * mask
    for copy in copies[n_kappa:n_field]:
        copy.wait()

    lane = lanes()

    def start_row(x, carry):
        for y in range(16):
            put(A, x, y, mul(row(G, x, y + 4), ld(F, x, y)))
        return carry

    lax.fori_loop(0, 16, start_row, 0, unroll=2)

    def sweep(src, dst, width, coarse):
        def one_row(x, reach):
            t = jnp.where(x >= 4, 1, 0) + jnp.where(x >= 12, 1, 0)
            for y, here, near in beside_rows(src, x, 4 - reach, 12 + reach, lane):
                new = add(scale(THIRD, here), mul(add(ld(F, x, y), near), row(G, x, y + 4)))
                if coarse:
                    jj = (1 if y >= 4 else 0) + (1 if y >= 12 else 0)
                    new = add(new, [c_ref[t * 3 + jj, :, k * L : (k + 1) * L] for k in range(CH)])
                put(dst, x, y, new)

        def inner(x, carry):
            one_row(x, width)
            return carry

        for a in range(1, width + 1):
            one_row(4 - a, width - a)
            one_row(11 + a, width - a)
        lax.fori_loop(4, 12, inner, 0, unroll=2)

    sweep(A, B, 3, True)
    sweep(B, A, 2, False)
    sweep(A, B, 1, False)
    for copy in copies[n_field:]:
        copy.wait()
    if first:
        fill_border(h_ref)
    nil = jnp.zeros((8, L), jnp.float32)

    def image_row(i, carry):
        fz, zq, ez = carry
        x = i + 4
        for y, here, near in beside_rows(B, x, 4, 12, lane):
            j = y - 4
            kappa = row(KY.at[1], i, j)
            image = [(6.0 + kappa[k]) * here[k] - near[k] for k in range(CH)]
            put(z_ref, i, j, here)
            put(q_ref, i, j, image)
            source = ld(F, x, y)
            fz = functools.reduce(lambda a, b: a + b, mul(source, here), fz)
            zq = functools.reduce(lambda a, b: a + b, mul(here, image), zq)
            if first:
                put(h_ref, i + 1, j + 1, mul(row(G, x, y + 4), image))
            else:
                ez = functools.reduce(lambda a, b: a + b, mul(ld(extra_ref, i, j), here), ez)
        return fz, zq, ez

    fz, zq, ez = lax.fori_loop(0, 8, image_row, (nil, nil, nil), unroll=2)
    if first:
        dots_ref[0] = fz
        dots_ref[1] = zq
        copies = run_copies(
            [
                (q_ref.at[0:8, pl.ds(4 * even, 4)], sends[0]),
                (q_ref.at[0:8, pl.ds(4 * odd, 4)], sends[1]),
            ]
            + [(q_ref.at[4 + i], sends[2].at[8 * i : 8 * i + 8]) for i in range(4)]
            + [(q_ref.at[i], sends[3].at[8 * i : 8 * i + 8]) for i in range(4)]
            + [
                (q_ref, q_out),
                (z_ref, z_out),
            ],
            sems,
        )
        gf_ref[0] = G[3, 8:16]
        gf_ref[1] = G[12, 8:16]
        for i in range(8):
            gf_ref[2, pl.ds(i, 1)] = G[4 + i, 7:8]
            gf_ref[3, pl.ds(i, 1)] = G[4 + i, 16:17]
        out_ref[...] = shares(
            h_ref,
            lambda i, j: ld(q_ref, i, j),
            lambda i, j: row(G, i + 4, j + 8),
            lambda f, n: row(gf_ref, f, n),
            rows_ref,
        )
        for copy in copies:
            copy.wait()
    else:
        copies = run_copies([(z_ref, z_out), (q_ref, q_out)], sems)
        total = [earlier_ref[0], earlier_ref[1], fz, zq, ez]
        packed = nil
        sub = lax.broadcasted_iota(jnp.int32, (8, L), 0)
        for k, part in enumerate(total):
            packed = jnp.where(lane == 8 * k + sub, jnp.sum(part, axis=1, keepdims=True), packed)
        packed = jnp.sum(packed, axis=0, keepdims=True)
        for n in range(2 * n_gy):
            dots_ref[n] = packed
        for copy in copies:
            copy.wait()


def combine_kernel(sums_ref, *refs):
    sources, outs = refs[:5], refs[5:7]
    b_ref, z_ref, q_ref, w_ref, v_ref = refs[7:12]
    x_keep, r_keep, in_sems, sems = refs[12:]
    fetched = [
        run_copies(
            [(src.at[2 * i : 2 * i + 2], dst.at[2 * i : 2 * i + 2]) for src, dst in zip(sources, refs[7:12])],
            in_sems,
            5 * i,
        )
        for i in range(4)
    ]
    sums = sums_ref[0]
    for n in range(1, sums_ref.shape[0]):
        sums = sums + sums_ref[n]
    sums = jnp.broadcast_to(sums, (8, L))
    sub = lax.broadcasted_iota(jnp.int32, (8, L), 0)
    bz, zq, qw, wv, bw = (
        jnp.sum(jnp.where(lanes() == 8 * k + sub, sums, 0.0), axis=1, keepdims=True) for k in range(5)
    )
    a0 = bz / zq
    e1 = bz - a0 * (bw + zq) + a0 * a0 * qw
    beta = e1 / bz
    z1q = zq - a0 * qw
    z1v = zq - 2.0 * a0 * qw + a0 * a0 * wv
    a1 = e1 / (z1v + 2.0 * beta * z1q + beta * beta * zq)
    cz = jnp.broadcast_to(a0 + a1 * (1.0 + beta), (8, CH * L))
    cw = jnp.broadcast_to(a1 * a0, (8, CH * L))
    copies = []
    for n in range(4):
        for copy in fetched[n]:
            copy.wait()
        for i in (2 * n, 2 * n + 1):
            for j in range(8):
                x_keep[i, j] = cz * z_ref[i, j] - cw * w_ref[i, j]
                r_keep[i, j] = b_ref[i, j] - cz * q_ref[i, j] + cw * v_ref[i, j]
        part = slice(2 * n, 2 * n + 2)
        copies += run_copies([(x_keep.at[part], outs[0].at[part]), (r_keep.at[part], outs[1].at[part])], sems, 2 * n)
    for copy in copies:
        copy.wait()


def shift(value, axes, sizes, steps):
    pairs = []
    total = 1
    for n in sizes:
        total *= n
    for flat in range(total):
        rest, target = flat, 0
        weight = 1
        for n, step in zip(reversed(sizes), reversed(steps)):
            at = rest % n
            rest //= n
            target += ((at + step) % n) * weight
            weight *= n
        pairs.append((flat, target))
    return lax.ppermute(value, axes, pairs)


VM = pl.BlockSpec(memory_space=pltpu.VMEM)
HB = pl.BlockSpec(memory_space=pl.ANY)


def solution(mesh):
    n_gx, n_gy = mesh.shape["gx"], mesh.shape["gy"]
    n_z = n_gx // 2
    fine = Mesh(mesh.devices.reshape(n_z, 2, n_gy), ALL)

    f32 = jnp.float32

    def shape(*dims):
        return jax.ShapeDtypeStruct(dims, f32)

    tile = shape(8, 8, 8, CH * L)
    y_face = shape(8, 4, 8, CH * L)

    even_pairs = [(n, n ^ 1) for n in range(n_gy)]
    odd_pairs = [(n, ((n - 1) ^ 1) + 1 if 0 < n < n_gy - 1 else n) for n in range(n_gy)]

    def along_gy(to_even, to_odd):
        return [lax.ppermute(to_even, "gy", even_pairs), lax.ppermute(to_odd, "gy", odd_pairs)]

    def after(first, then):
        return pl.pallas_call(
            pass_kernel,
            out_shape=[shape(*v.shape) for v in then],
            in_specs=[HB] * (len(first) + len(then)),
            out_specs=[HB] * len(then),
            input_output_aliases={len(first) + n: n for n in range(len(then))},
            compiler_params=WHOLE,
            name="pass_on",
        )(*first, *then)

    def along_gx(to_high, to_low):
        return [shift(to_high, GX, (n_gx,), (1,)), shift(to_low, GX, (n_gx,), (-1,))]

    def exchange(own, faces, messages, more):
        low = shift(own, ("z",), (n_z,), (1,))
        high = shift(own, ("z",), (n_z,), (-1,))
        cells = along_gx(*after((low, high), messages))
        size = CORNERS if more else KAPPA_AT
        part = pltpu.VMEM((size, 8, CH * L), f32)
        out, to_high, to_low = pl.pallas_call(
            functools.partial(merge_kernel, bool(more), n_z, n_gy),
            out_shape=[shape(2 * n_gy, 9, 1, L)] + [shape(size, 8, CH * L)] * 2,
            in_specs=[VM] * 3 + [HB] * (2 + len(more)),
            out_specs=[VM, HB, HB],
            scratch_shapes=[part, part, pltpu.SemaphoreType.DMA((20,))],
            compiler_params=GRANT,
            name="merge_shares",
        )(own, low, high, *(f.reshape(32, 8, CH * L) for f in faces), *more)
        corners = along_gx(to_high, to_low)
        return lax.all_to_all(out, SLAB2, 0, 0), cells + corners

    def body(b, kappa, inverse):
        around = [
            shift(kappa, GX, (n_gx,), (1,)),
            shift(kappa, GX, (n_gx,), (-1,)),
            *along_gy(kappa, kappa),
        ]
        packed = pl.pallas_call(
            functools.partial(pack_kernel, n_gy),
            out_shape=[y_face, y_face] + [shape(LAST, 8, CH * L)] * 2,
            in_specs=[HB, HB],
            out_specs=[HB] * 4,
            scratch_shapes=[
                pltpu.VMEM((64, 8, CH * L), f32),
                pltpu.VMEM((3, 8, CH * L), f32),
                pltpu.SemaphoreType.DMA((7,)),
                pltpu.SemaphoreType.DMA((20,)),
            ],
            compiler_params=WHOLE,
            name="pack_faces",
        )(b.reshape(64, 8, CH * L), inverse)
        behind = after(around, packed[:2])
        b_faces = along_gy(*behind)
        own = pl.pallas_call(
            functools.partial(first_shares_kernel, n_gx, n_gy),
            out_shape=shape(9, L),
            in_specs=[HB] * 6,
            out_specs=VM,
            scratch_shapes=[
                pltpu.VMEM((10, 10, 8, CH * L), f32),
                pltpu.VMEM((8, 8, CH * L), f32),
                pltpu.VMEM((4, 8, CH * L), f32),
                pltpu.VMEM((8, 8, CH * L), f32),
                pltpu.VMEM((8, 8, 8, CH * L), f32),
                pltpu.VMEM((2, 8, CH * L), f32),
                pltpu.VMEM((3, 8, 8, CH * L), f32),
                pltpu.SemaphoreType.DMA((9,)),
            ],
            compiler_params=GRANT,
            name="first_shares",
        )(b, kappa, *around)

        def cycle(first, field, faces, messages, b_messages, received, more):
            outs = [tile, tile]
            out_specs = [HB, HB, VM]
            if first:
                outs += [shape(2, 8, L), shape(9, L), y_face, y_face]
                outs += [shape(CELLS, 8, CH * L)] * 2
                out_specs += [VM, HB, HB, HB, HB]
            else:
                outs += [shape(2 * n_gy, 1, L)]
            big = pltpu.VMEM((16, 16, 8, CH * L), f32)
            own_tile = pltpu.VMEM((8, 8, 8, CH * L), f32)
            return pl.pallas_call(
                functools.partial(cycle_kernel, first, n_gx, n_gy),
                out_shape=outs,
                in_specs=[HB] * 18 + ([HB, VM] if more else []),
                out_specs=out_specs,
                scratch_shapes=[
                    big,
                    big,
                    big,
                    pltpu.VMEM((16, 24, CH * L), f32),
                    pltpu.VMEM((2, 6, 8, CH * L), f32),
                    pltpu.VMEM((2, 4, 8, CH * L), f32),
                    pltpu.VMEM((3, 8, 8, CH * L), f32),
                    pltpu.VMEM((3, 48, 16 * n_gy), f32),
                    pltpu.VMEM((9, 8, CH * L), f32),
                    pltpu.VMEM((10, 10, 8, CH * L), f32),
                    pltpu.VMEM((4, 8, CH * L), f32),
                    pltpu.VMEM((8, 8, CH * L), f32),
                    own_tile,
                    own_tile,
                    own_tile,
                    pltpu.VMEM((2 * n_gy, 9, 1, L), f32),
                    pltpu.SemaphoreType.DMA((52,)),
                ],
                compiler_params=GRANT,
                name="first_cycle" if first else "second_cycle",
            )(field, *faces, *messages, *b_messages, kappa, *around, inverse, received, *more)

        received, b_messages = exchange(own, b_faces, packed[2:], around[2:])
        z0, q0, dots, own, *sends = cycle(True, b, b_faces, b_messages, b_messages, received, [])
        q_faces = along_gy(*sends[:2])
        received, messages = exchange(own, q_faces, sends[2:], [])
        w0, v0, packed = cycle(False, q0, q_faces, messages, b_messages, received, [b, dots])

        near_sum = jnp.sum(lax.all_to_all(packed, SLAB2, 0, 0), axis=0)
        sums = lax.all_to_all(jnp.broadcast_to(near_sum, (n_z, 1, L)), "z", 0, 0)
        return pl.pallas_call(
            combine_kernel,
            out_shape=[tile, tile],
            in_specs=[VM] + [HB] * 5,
            out_specs=[HB, HB],
            scratch_shapes=[pltpu.VMEM((8, 8, 8, CH * L), f32)] * 7
            + [pltpu.SemaphoreType.DMA((20,)), pltpu.SemaphoreType.DMA((8,))],
            compiler_params=GRANT,
            name="combine",
        )(sums, b, z0, q0, w0, v0)

    field = P(GX, "gy", None, None)
    return jax.shard_map(
        body,
        mesh=fine,
        in_specs=(field, P(GX, "gy", None), P(GX, None)),
        out_specs=(field, field),
        check_vma=False,
    )
```
